256 devices in a mesh: px: 16 (over z, core), py: 16 (over y, x).
Axes of the slice: x: 4, y: 4, z: 8, core: 2. Of those that a mesh axis runs over, the one named last changes fastest.
Arguments:
- right_side: float32 [256, 512, 512], P('px', 'py'), may hold values from -10 to 10
- shift: float32 [256, 512, 512], P('px', 'py'), may hold values from 0.5 to 4
- coarse_inverse: float32 [2048, 2048], P(('px', 'py')), may hold values from -1 to 1, as said below
Outputs:
- solution_field: float32 [256, 512, 512], P('px', 'py')
- residual: float32 [256, 512, 512], P('px', 'py')
The draws below stay inside these ranges and needn't reach their ends.
Inputs may be any that keep to these rules, and one draw needn't show every extreme that they name: `coarse_inverse`: exactly symmetric and positive definite.
All inputs are finite; a program needn't handle non-finite values.
Results may differ from the reference program's by a relative error of at most 0.00022.
Values sent between devices are 32-bit elements; how exact they have to be, the bound alone decides.
No kernel may reach another device: no remote copies, remote signals or barrier semaphores. Data moves between devices by JAX's collectives and lax.ppermute only.
A program may use at most 64 MiB of HBM per device.

```python
import math
import jax
import jax.numpy as jnp
from jax import lax

CX = 16
CY = 32
NZ = 512
AGG_DEV = 8
ITERS = 2
SWEEPS = 3
NX = 256
NY = 512
K = 2048
N_PX = 16
N_PY = 16


def draw_right_side(key, part):
    key = jax.random.fold_in(key, 3)
    rough_key, phase_key = jax.random.split(key)
    phases = jax.random.uniform(phase_key, (3,), jnp.float32) * (2.0 * math.pi)
    first = jnp.arange(NX, dtype=jnp.float32) / NX
    second = jnp.arange(NY, dtype=jnp.float32) / NY
    third = jnp.arange(NZ, dtype=jnp.float32) / NZ
    ramp = (0.6 + 1.2 * first)[:, None, None]
    wave_x = jnp.cos(2.0 * math.pi * first + phases[0])[:, None, None]
    wave_z = jnp.cos(4.0 * math.pi * third + phases[1])[None, None, :]
    wave_y = jnp.cos(6.0 * math.pi * second + phases[2])[None, :, None]
    smooth = 1.5 * wave_x * wave_z + wave_y
    rough = jnp.clip(jax.random.normal(rough_key, (NX, NY, NZ), jnp.float32), -4.0, 4.0)
    return ramp * rough + smooth


def draw_coarse_inverse(key, part):
    key = jax.random.fold_in(key, 7)
    noise_key, diag_key = jax.random.split(key)
    noise = jax.random.normal(noise_key, (K, K), jnp.float32)
    mixed = (noise + noise.T) * (0.15 / math.sqrt(2.0 * K))
    mixed = jnp.clip(mixed, -0.5, 0.5)
    diag = jax.random.uniform(diag_key, (K,), jnp.float32, 0.4, 0.7)
    rows = jnp.arange(K)[:, None]
    cols = jnp.arange(K)[None, :]
    return jnp.where(rows == cols, diag[:, None], mixed)


def level_of(own_key, extent, cuts, low, high):
    def one(position, parts):
        draws = jax.random.uniform(jax.random.fold_in(jax.random.fold_in(own_key, 6), position), (parts,), jnp.float32, low / len(cuts), high / len(cuts))
        return jnp.repeat(jnp.exp(draws), extent[position] // parts).reshape((-1,) + (1,) * (len(extent) - position - 1))

    factor_of = one(*cuts[0])
    for cut in cuts[1:]:
        factor_of = factor_of * one(*cut)
    return factor_of


def setup_inputs(seed: int = 0) -> dict:
    arg_keys = jax.random.split(jax.random.key(seed), 4)
    return {
        "right_side": draw_right_side(jax.random.fold_in(arg_keys[3], 71), 0),
        "shift": jnp.clip(jnp.exp(math.log(4.0) - 2.0794415 * jax.random.uniform(arg_keys[1], (NX, NY, NZ), jnp.float32) ** level_of(arg_keys[1], (NX, NY, NZ), ((0, 16), (1, 16)), -0.2, 0.2)), 0.5, 4.0),
        "coarse_inverse": draw_coarse_inverse(jax.random.fold_in(arg_keys[3], 71), 0),
    }


def box_sum(padded):
    total = padded[:-2] + padded[1:-1] + padded[2:]
    total = total[:, :-2] + total[:, 1:-1] + total[:, 2:]
    total = total[:, :, :-2] + total[:, :, 1:-1] + total[:, :, 2:]
    return total


def operate(field, shift):
    return (27.0 + shift) * field - box_sum(jnp.pad(field, 1))


def coarse_means(field):
    slab = NZ // AGG_DEV
    shaped = field.reshape(N_PX, CX, N_PY, CY, AGG_DEV, slab)
    return jnp.mean(shaped, axis=(1, 3, 5)).reshape(-1)


def prolong(values):
    slab = NZ // AGG_DEV
    shaped = values.reshape(N_PX, 1, N_PY, 1, AGG_DEV, 1)
    full = jnp.broadcast_to(shaped, (N_PX, CX, N_PY, CY, AGG_DEV, slab))
    return full.reshape(N_PX * CX, N_PY * CY, NZ)


def precondition(resid, shift, coarse_inverse):
    scale = 26.0 + shift
    smooth = resid / scale
    for sweep in range(SWEEPS - 1):
        smooth = smooth + (resid - operate(smooth, shift)) / scale
    values = jnp.dot(coarse_inverse, coarse_means(resid), precision=lax.Precision.HIGHEST)
    return smooth + prolong(values)


def reference(right_side, shift, coarse_inverse):
    solution_field = jnp.zeros_like(right_side)
    residual = right_side
    zvalue = precondition(residual, shift, coarse_inverse)
    direction = zvalue
    rz_now = jnp.sum(residual * zvalue)
    for step in range(ITERS):
        image = operate(direction, shift)
        alpha = rz_now / jnp.sum(direction * image)
        solution_field = solution_field + alpha * direction
        residual = residual - alpha * image
        if step + 1 < ITERS:
            zvalue = precondition(residual, shift, coarse_inverse)
            rz_next = jnp.sum(residual * zvalue)
            direction = zvalue + (rz_next / rz_now) * direction
            rz_now = rz_next
    return solution_field, residual
```

```python
import functools

import jax
import jax.numpy as jnp
from jax import lax
from jax.experimental import pallas as pl
from jax.experimental.pallas import tpu as pltpu
from jax.sharding import PartitionSpec as P

CX, CY, NZ = 16, 32, 512
AGG = 8
SLAB = NZ // AGG
CELLS = CX * CY * SLAB
W = 3
XE = CX + 2 * W
Y0 = 8
YE = CY + 2 * Y0
LANES = 128
F32 = jnp.float32
HIGH = lax.Precision.HIGHEST


def lane_sum(plane):
    lane = lax.broadcasted_iota(jnp.int32, (plane.shape[0], LANES), 1)
    parts = [plane[:, k * LANES : (k + 1) * LANES] for k in range(NZ // LANES)]
    up = [pltpu.roll(p, 1, axis=1) for p in parts]
    down = [pltpu.roll(p, LANES - 1, axis=1) for p in parts]
    zero = jnp.zeros_like(parts[0])
    out = []
    for k, p in enumerate(parts):
        left = jnp.where(lane == 0, up[k - 1] if k else zero, up[k])
        right = jnp.where(
            lane == LANES - 1, down[k + 1] if k + 1 < len(parts) else zero, down[k]
        )
        out.append(left + p + right)
    return jnp.concatenate(out, axis=1)


def plane_box(plane):
    rows = plane.shape[0]
    plane = plane + pltpu.roll(plane, 1, axis=0) + pltpu.roll(plane, rows - 1, axis=0)
    return lane_sum(plane)


def neighbours(ref, i):
    mid = ref[i]
    return plane_box(ref[i - 1] + mid + ref[i + 1]) - mid


def each(low, high, body):
    lax.fori_loop(low, high, lambda i, carry: (body(i), carry)[1], 0)


def total(x):
    return jnp.sum(x, keepdims=True)


def slab_matrix(offset):
    cell = lax.broadcasted_iota(jnp.int32, (NZ, LANES), 0)
    lane = lax.broadcasted_iota(jnp.int32, (NZ, LANES), 1)
    return jnp.where(cell // SLAB + offset == lane, 1.0, 0.0).astype(F32)


def spread_matrix():
    lane = lax.broadcasted_iota(jnp.int32, (LANES, NZ), 0)
    cell = lax.broadcasted_iota(jnp.int32, (LANES, NZ), 1)
    return jnp.where(cell // SLAB == lane, 1.0, 0.0).astype(F32)


def slab_sums(acc, offset):
    return jnp.dot(
        jnp.sum(acc, axis=0, keepdims=True), slab_matrix(offset),
        precision=HIGH, preferred_element_type=F32,
    )


def first_lanes(x):
    lane = lax.broadcasted_iota(jnp.int32, x.shape, 1)
    return jnp.where(lane < AGG, x, 0.0)


def coarse_rows(columns, vector):
    prod = lax.dot_general(
        columns, vector, (((0,), (0,)), ((), ())), precision=HIGH,
        preferred_element_type=F32,
    )
    row = lax.broadcasted_iota(jnp.int32, prod.shape, 0)
    lane = lax.broadcasted_iota(jnp.int32, prod.shape, 1)
    each_row = jnp.sum(
        jnp.where((row & (AGG - 1)) == lane, prod, 0.0), axis=1, keepdims=True
    )
    return jnp.sum(
        jnp.where((row // AGG) == lane, each_row, 0.0), axis=0, keepdims=True
    )


def coarse_operator(c, shift_sums, n_py):
    n = c.shape[0]
    row = lax.broadcasted_iota(jnp.int32, c.shape, 0)
    inner = row & (n_py - 1)
    t = (3.0 * SLAB - 2.0) * c + first_lanes(
        pltpu.roll(c, 1, axis=1) + pltpu.roll(c, LANES - 1, axis=1)
    )
    t = (
        (3.0 * CY - 2.0) * t
        + jnp.where(inner == 0, 0.0, pltpu.roll(t, 1, axis=0))
        + jnp.where(inner == n_py - 1, 0.0, pltpu.roll(t, n - 1, axis=0))
    )
    t = (
        (3.0 * CX - 2.0) * t
        + jnp.where(row < n_py, 0.0, pltpu.roll(t, n_py, axis=0))
        + jnp.where(row >= n - n_py, 0.0, pltpu.roll(t, n - n_py, axis=0))
    )
    return (27.0 * CELLS + shift_sums) * c - t


def assemble(ref, own, px_lo, px_hi, py_lo, py_hi, base=0):
    ref[...] = jnp.zeros_like(ref)
    ref[W : W + CX, Y0 : Y0 + CY] = own[...]
    ref[:W, Y0 : Y0 + CY] = px_lo[...]
    ref[W + CX :, Y0 : Y0 + CY] = px_hi[...]
    for i in range(XE):
        at = base + i * W
        ref[i, Y0 - W : Y0] = py_lo[at : at + W]
        ref[i, Y0 + CY : Y0 + CY + W] = py_hi[at : at + W]


def own_rows(plane):
    return plane[Y0 : Y0 + CY]


def smooth(rref, iref, zref, yref):
    def first(i):
        zref[i] = rref[i] * iref[i]

    def second(i):
        yref[i] = (rref[i] + neighbours(zref, i)) * iref[i]

    def third(i):
        zref[i] = (rref[i] + neighbours(yref, i)) * iref[i]

    each(0, XE, first)
    each(1, XE - 1, second)
    each(2, XE - 2, third)


def coarse_planes(where, cref, n_px, n_py, rows9):
    a, b = where[0], where[1]
    rows9[...] = jnp.zeros_like(rows9)
    for da in (-1, 0, 1):
        for db in (-1, 0, 1):
            aa, bb = a + da, b + db
            inside = (aa >= 0) & (aa < n_px) & (bb >= 0) & (bb < n_py)
            k = jnp.clip(aa, 0, n_px - 1) * n_py + jnp.clip(bb, 0, n_py - 1)
            at = (da + 1) * 3 + db + 1
            rows9[at : at + 1] = jnp.where(inside, cref[pl.ds(k, 1), :], 0.0)
    spread = jnp.dot(rows9[...], spread_matrix(), precision=HIGH, preferred_element_type=F32)
    t = lax.broadcasted_iota(jnp.int32, (YE, NZ), 0)
    planes = []
    for da in range(3):
        lo, mid, hi = (spread[da * 3 + k : da * 3 + k + 1] for k in range(3))
        planes.append(jnp.where(t < Y0, lo, jnp.where(t < Y0 + CY, mid, hi)))
    return planes, [plane_box(p) for p in planes]


def box_plane(boxes, i):
    x = i - W
    lo, mid, hi = boxes
    if x <= -2:
        return 3.0 * lo
    if x == -1:
        return 2.0 * lo + mid
    if x == 0:
        return lo + 2.0 * mid
    if x < CX - 1:
        return 3.0 * mid
    if x == CX - 1:
        return 2.0 * mid + hi
    if x == CX:
        return mid + 2.0 * hi
    return 3.0 * hi


def block_plane(planes, i):
    return planes[0 if i < W else 1 if i < W + CX else 2]


def kernel_a(where, r, s, rlo, rhi, slo, shi, ylo, yhi, columns, g1,
             rext, sext, iext, u, v, row, zref, yref, accv, accs, *, n_px, n_py):
    assemble(rext, r, rlo, rhi, ylo, yhi)
    assemble(sext, s, slo, shi, ylo, yhi, XE * W)
    a, b = where[0], where[1]
    t = lax.broadcasted_iota(jnp.int32, (YE, NZ), 0)
    low = jnp.where(b > 0, Y0 - W, Y0)
    high = jnp.where(b < n_py - 1, Y0 + CY + W, Y0 + CY)
    first = jnp.where(a > 0, 0, W)
    last = jnp.where(a < n_px - 1, XE, W + CX)
    inside = (t >= low) & (t < high)

    def invert(i):
        keep = inside & (i >= first) & (i < last)
        iext[i] = jnp.where(keep, 1.0 / (26.0 + sext[i]), 0.0)

    each(0, XE, invert)
    smooth(rext, iext, zref, yref)
    accv[...] = jnp.zeros_like(accv)
    accs[...] = jnp.zeros_like(accs)

    def apply(i, carry):
        ru, uv = carry
        uu = own_rows(zref[i])
        ss = own_rows(sext[i])
        vv = (26.0 + ss) * uu - own_rows(neighbours(zref, i))
        u[i - W] = uu
        v[i - W] = vv
        accv[...] += vv
        accs[...] += ss
        return ru + own_rows(rext[i]) * uu, uv + uu * vv

    zero = jnp.zeros((CY, NZ), F32)
    ru, uv = lax.fori_loop(W, W + CX, apply, (zero, zero))
    c = coarse_rows(columns[...], g1[...])
    lane = lax.broadcasted_iota(jnp.int32, (1, LANES), 1)
    out = c + slab_sums(accv[...], AGG) * (1.0 / CELLS) + slab_sums(accs[...], 2 * AGG)
    out = out + jnp.where(lane == 24, total(ru), 0.0) + jnp.where(lane == 25, total(uv), 0.0)
    row[...] = jnp.broadcast_to(out, row.shape)


def kernel_b(where, rext, sext, iext, v, vlo, vhi, ylo, yhi, columns, g1, g2,
             r1o, uo, vo, qo, row, scal, rref, qref, zref, yref, cref, rows9, accv, *,
             n_px, n_py):
    g = g2[...]
    m = first_lanes(g1[...])
    c = first_lanes(g)
    w = first_lanes(pltpu.roll(g, LANES - AGG, axis=1))
    shifts = first_lanes(pltpu.roll(g, LANES - 2 * AGG, axis=1))
    lane = lax.broadcasted_iota(jnp.int32, g.shape, 1)
    tc = coarse_operator(c, shifts, n_py)
    rz = total(jnp.where(lane == 24, g, 0.0) + CELLS * (m * c))
    curv = total(jnp.where(lane == 25, g, 0.0) + (2.0 * CELLS) * (c * w) + c * tc)
    alpha = rz / curv
    e = w + tc * (1.0 / CELLS)
    mnew = m - alpha * e
    cref[...] = c
    cnew = coarse_rows(columns[...], mnew)
    planes, boxes = coarse_planes(where, cref, n_px, n_py, rows9)
    assemble(qref, v, vlo, vhi, ylo, yhi)

    def image(i, pc, bc):
        q = qref[i] + (27.0 + sext[i]) * pc - bc
        qref[i] = q
        rref[i] = rext[i] - alpha * q

    for i in (0, 1, 2, 3, W + CX - 1, W + CX, W + CX + 1, W + CX + 2):
        image(i, block_plane(planes, i), box_plane(boxes, i))
    pc, bc = planes[1], 3.0 * boxes[1]
    each(W + 1, W + CX - 1, lambda i: image(i, pc, bc))
    smooth(rref, iext, zref, yref)
    accv[...] = jnp.zeros_like(accv)

    def apply(i, carry):
        ru, uv, uq = carry
        uu = own_rows(zref[i])
        rr = own_rows(rref[i])
        qq = own_rows(qref[i])
        vv = (26.0 + own_rows(sext[i])) * uu - own_rows(neighbours(zref, i))
        uo[i - W] = uu
        vo[i - W] = vv
        r1o[i - W] = rr
        qo[i - W] = qq
        accv[...] += vv
        return ru + rr * uu, uv + uu * vv, uq + uu * qq

    zero = jnp.zeros((CY, NZ), F32)
    ru, uv, uq = lax.fori_loop(W, W + CX, apply, (zero, zero, zero))
    me = where[0] * n_py + where[1]
    cref[...] = e
    e_own = cref[pl.ds(me, 1), :]
    cref[...] = mnew
    m_own = cref[pl.ds(me, 1), :]
    lane = lax.broadcasted_iota(jnp.int32, (1, LANES), 1)
    out = cnew + slab_sums(accv[...], AGG) * (1.0 / CELLS)
    out = out + jnp.where(lane == 24, total(ru) + CELLS * total(m_own * cnew), 0.0)
    out = out + jnp.where(lane == 25, total(uv), 0.0)
    out = out + jnp.where(lane == 26, total(uq) + CELLS * total(e_own * cnew), 0.0)
    row[...] = jnp.broadcast_to(out, row.shape)
    at = lax.broadcasted_iota(jnp.int32, (8, LANES), 0)
    scal[...] = jnp.where(at == 0, rz, jnp.where(at == 1, curv, alpha))


def kernel_c(where, s, u, r1, un, vn, q, g2, g3, scal, x, r2, cref, rows9, *, n_px, n_py):
    g = g3[...]
    c = first_lanes(g)
    w = first_lanes(pltpu.roll(g, LANES - AGG, axis=1))
    shifts = first_lanes(pltpu.roll(g2[...], LANES - 2 * AGG, axis=1))
    lane = lax.broadcasted_iota(jnp.int32, g.shape, 1)
    tc = coarse_operator(c, shifts, n_py)
    rz, curv, alpha = scal[0:1, 0:1], scal[1:2, 0:1], scal[2:3, 0:1]
    rz1 = total(jnp.where(lane == 24, g, 0.0))
    zaz = total(jnp.where(lane == 25, g, 0.0) + (2.0 * CELLS) * (c * w) + c * tc)
    zq = total(jnp.where(lane == 26, g, 0.0))
    beta = rz1 / rz
    alpha2 = rz1 / (zaz + 2.0 * beta * zq + beta * beta * curv)
    first = alpha + alpha2 * beta
    me = where[0] * n_py + where[1]
    cref[...] = c
    planes, boxes = coarse_planes(where, cref, n_px, n_py, rows9)
    c_old = jnp.dot(
        jnp.broadcast_to(first_lanes(g2[pl.ds(me, 1), :]), (8, LANES)), spread_matrix(),
        precision=HIGH, preferred_element_type=F32,
    )
    pc = own_rows(planes[1])
    base = first * c_old[0:1] + alpha2 * pc

    def finish(i, bc):
        j = i - W
        x[j] = first * u[j] + alpha2 * un[j] + base
        image = vn[j] + (27.0 + s[j]) * pc - bc + beta * q[j]
        r2[j] = r1[j] - alpha2 * image

    for i in (W, W + CX - 1):
        finish(i, own_rows(box_plane(boxes, i)))
    bc = own_rows(3.0 * boxes[1])
    each(W + 1, W + CX - 1, lambda i: finish(i, bc))


VMEM = pl.BlockSpec(memory_space=pltpu.VMEM)
SMEM = pl.BlockSpec(memory_space=pltpu.SMEM)


def call(body, n_in, outs, scratch, name, **sizes):
    return pl.pallas_call(
        functools.partial(body, **sizes),
        in_specs=[SMEM] + [VMEM] * (n_in - 1),
        out_specs=[VMEM] * len(outs),
        out_shape=[jax.ShapeDtypeStruct(o, F32) for o in outs],
        scratch_shapes=[pltpu.VMEM(x, F32) for x in scratch],
        compiler_params=pltpu.CompilerParams(vmem_limit_bytes=48 * 1024 * 1024),
        name=name,
    )


EXT = (XE, YE, NZ)
OWN = (CX, CY, NZ)


def to_next(x, axis, n):
    return lax.ppermute(x, axis, [(i, i + 1) for i in range(n - 1)])


def to_previous(x, axis, n):
    return lax.ppermute(x, axis, [(i + 1, i) for i in range(n - 1)])


def halo(fields, n_px, n_py):
    lo = to_next(jnp.concatenate([f[-W:] for f in fields]), "px", n_px)
    hi = to_previous(jnp.concatenate([f[:W] for f in fields]), "px", n_px)
    los = [lo[k * W : (k + 1) * W] for k in range(len(fields))]
    his = [hi[k * W : (k + 1) * W] for k in range(len(fields))]

    def side(rows):
        return jnp.concatenate(
            [p[:, rows] for l, f, h in zip(los, fields, his) for p in (l, f, h)]
        ).reshape(len(fields) * XE * W, NZ)

    ylo = to_next(side(slice(CY - W, CY)), "py", n_py)
    yhi = to_previous(side(slice(0, W)), "py", n_py)
    return los, his, ylo, yhi


def gather(row, n):
    return lax.all_to_all(
        jnp.broadcast_to(row[:1], (n, LANES)), ("px", "py"), 0, 0, tiled=True
    )


def per_device(right_side, shift, coarse_inverse, *, n_px, n_py):
    n = n_px * n_py
    sizes = dict(n_px=n_px, n_py=n_py)
    where = jnp.stack([lax.axis_index("px"), lax.axis_index("py")]).astype(jnp.int32)
    columns = coarse_inverse.reshape(AGG, n, AGG).transpose(1, 0, 2).reshape(n, AGG * AGG)
    sums = jnp.sum(jnp.sum(right_side, axis=(0, 1)).reshape(AGG, SLAB), axis=1)
    g1 = gather(jnp.pad(sums / CELLS, (0, LANES - AGG))[None], n)
    (rlo, slo), (rhi, shi), ylo, yhi = halo((right_side, shift), n_px, n_py)
    rext, sext, iext, u, v, row = call(
        kernel_a, 11, [EXT, EXT, EXT, OWN, OWN, (8, LANES)],
        [EXT, EXT, (CY, NZ), (CY, NZ)], "first", **sizes,
    )(where, right_side, shift, rlo, rhi, slo, shi, ylo, yhi, columns, g1)
    g2 = gather(row, n)
    (vlo,), (vhi,), ylo, yhi = halo((v,), n_px, n_py)
    r1, un, vn, q, row, scal = call(
        kernel_b, 12, [OWN, OWN, OWN, OWN, (8, LANES), (8, LANES)],
        [EXT, EXT, EXT, EXT, (n, LANES), (16, LANES), (CY, NZ)], "second", **sizes,
    )(where, rext, sext, iext, v, vlo, vhi, ylo, yhi, columns, g1, g2)
    g3 = gather(row, n)
    return tuple(
        call(
            kernel_c, 10, [OWN, OWN], [(n, LANES), (16, LANES)], "third", **sizes
        )(where, shift, u, r1, un, vn, q, g2, g3, scal)
    )


def solution(mesh):
    n_px, n_py = mesh.shape["px"], mesh.shape["py"]
    placed = (P("px", "py", None), P("px", "py", None), P(("px", "py"), None))
    return jax.shard_map(
        functools.partial(per_device, n_px=n_px, n_py=n_py),
        mesh=mesh,
        in_specs=placed,
        out_specs=(P("px", "py", None), P("px", "py", None)),
        check_vma=False,
    )
```

```python
import functools

import jax
import jax.numpy as jnp
from jax import lax
from jax.experimental import pallas as pl
from jax.experimental.pallas import tpu as pltpu
from jax.sharding import PartitionSpec as P

CX, CY, NZ = 16, 32, 512
AGG = 8
SLAB = NZ // AGG
CELLS = CX * CY * SLAB
H = 6
V = 3
T = 8
XE = CX + 2 * H
XV = CX + 2 * V
YE = CY + 2 * T
TILES = YE // T
LANES = 128
F32 = jnp.float32
HIGH = lax.Precision.HIGHEST
OWN = (CX, CY, NZ)
EXT = (XE, YE, NZ)
MID = (XV, YE, NZ)


def tile(t):
    return slice(t * T, (t + 1) * T)


def iota(shape, axis):
    return lax.broadcasted_iota(jnp.int32, shape, axis)


def chunks(row):
    return [row[:, k * LANES : (k + 1) * LANES] for k in range(NZ // LANES)]


def lane_sum(rows):
    lane = iota((rows.shape[0], LANES), 1)
    parts = chunks(rows)
    up = [pltpu.roll(p, 1, axis=1) for p in parts]
    down = [pltpu.roll(p, LANES - 1, axis=1) for p in parts]
    zero = jnp.zeros_like(parts[0])
    out = []
    for k, p in enumerate(parts):
        left = jnp.where(lane == 0, up[k - 1] if k else zero, up[k])
        right = jnp.where(
            lane == LANES - 1, down[k + 1] if k + 1 < len(parts) else zero, down[k]
        )
        out.append(left + p + right)
    return jnp.concatenate(out, axis=1)


def tile_boxes(xsum, tiles):
    row = iota((T, NZ), 0)
    have = {}

    def get(t):
        if t not in have:
            x = xsum(t)
            have[t] = (x, pltpu.roll(x, 1, axis=0), pltpu.roll(x, T - 1, axis=0))
        return have[t]

    for t in tiles:
        x, up, down = get(t)
        if t > 0:
            up = jnp.where(row == 0, get(t - 1)[1], up)
        if t < TILES - 1:
            down = jnp.where(row == T - 1, get(t + 1)[2], down)
        yield t, lane_sum(up + x + down)


def neighbours(ref, i, tiles):
    def xsum(t):
        return ref[i - 1, tile(t)] + ref[i, tile(t)] + ref[i + 1, tile(t)]

    for t, box in tile_boxes(xsum, tiles):
        mid = ref[i, tile(t)]
        yield t, box - mid, mid


def plane_box(plane):
    parts = [box for _, box in tile_boxes(lambda t: plane[tile(t)], range(TILES))]
    return jnp.concatenate(parts, axis=0)


def each(low, high, body):
    lax.fori_loop(low, high, lambda i, carry: (body(i), carry)[1], 0)


def total(x):
    return jnp.sum(x, keepdims=True)


def fold(rows):
    a, b, c, d = chunks(rows)
    return (a + b) + (c + d)


def exact_dot(a, b):
    return jnp.dot(a, b, precision=HIGH, preferred_element_type=F32)


def slab_sums(acc, offset):
    cell, lane = iota((NZ, LANES), 0), iota((NZ, LANES), 1)
    pick = jnp.where(cell // SLAB + offset == lane, 1.0, 0.0).astype(F32)
    return jnp.sum(exact_dot(acc, pick), axis=0, keepdims=True)


def spread(rows):
    lane, cell = iota((LANES, NZ), 0), iota((LANES, NZ), 1)
    return exact_dot(rows, jnp.where(cell // SLAB == lane, 1.0, 0.0).astype(F32))


def line_up(rows, offset, n_py):
    width = n_py * AGG
    src, dst = iota((LANES, width), 0), iota((LANES, width), 1)
    repeat = jnp.where((dst & (AGG - 1)) + offset == src, 1.0, 0.0).astype(F32)
    wide = exact_dot(rows, repeat)
    row, lane = iota(wide.shape, 0), iota(wide.shape, 1)
    wide = jnp.where((row & (n_py - 1)) == lane // AGG, wide, 0.0)
    return jnp.sum(wide.reshape(rows.shape[0] // n_py, n_py, width), axis=1)


def coarse_rows(inverse, vector):
    n, width = vector.shape
    acc = jnp.zeros((AGG, width), F32)
    for k in range(n):
        acc = acc + inverse[:, k * width : (k + 1) * width] * vector[k : k + 1]
    column = jnp.sum(acc, axis=1, keepdims=True)
    row, lane = iota((AGG, LANES), 0), iota((AGG, LANES), 1)
    return jnp.sum(jnp.where(row == lane, column, 0.0), axis=0, keepdims=True)


def coarse_operator(c, shift_sums):
    n, width = c.shape
    row, lane = iota(c.shape, 0), iota(c.shape, 1)
    slab = lane & (AGG - 1)
    t = (
        (3.0 * SLAB - 2.0) * c
        + jnp.where(slab == 0, 0.0, pltpu.roll(c, 1, axis=1))
        + jnp.where(slab == AGG - 1, 0.0, pltpu.roll(c, width - 1, axis=1))
    )
    t = (
        (3.0 * CY - 2.0) * t
        + jnp.where(lane < AGG, 0.0, pltpu.roll(t, AGG, axis=1))
        + jnp.where(lane >= width - AGG, 0.0, pltpu.roll(t, width - AGG, axis=1))
    )
    t = (
        (3.0 * CX - 2.0) * t
        + jnp.where(row == 0, 0.0, pltpu.roll(t, 1, axis=0))
        + jnp.where(row == n - 1, 0.0, pltpu.roll(t, n - 1, axis=0))
    )
    return (27.0 * CELLS + shift_sums) * c - t


def own_part(vector, where, ref):
    ref[...] = vector
    mine = ref[pl.ds(where[0], 1), :]
    lane = iota(mine.shape, 1)
    mine = jnp.where(lane // AGG == where[1], mine, 0.0)
    src, dst = iota((mine.shape[1], LANES), 0), iota((mine.shape[1], LANES), 1)
    pick = jnp.where((src & (AGG - 1)) == dst, 1.0, 0.0).astype(F32)
    return exact_dot(jnp.broadcast_to(mine, (T, mine.shape[1])), pick)[:1]


def coarse_planes(where, gathered, n_px, n_py, rows9):
    a, b = where[0], where[1]
    rows9[...] = jnp.zeros_like(rows9)
    for da in (-1, 0, 1):
        for db in (-1, 0, 1):
            aa, bb = a + da, b + db
            inside = (aa >= 0) & (aa < n_px) & (bb >= 0) & (bb < n_py)
            k = jnp.clip(aa, 0, n_px - 1) * n_py + jnp.clip(bb, 0, n_py - 1)
            at = (da + 1) * 3 + db + 1
            rows9[at : at + 1] = jnp.where(inside, gathered[pl.ds(k, 1), :], 0.0)
    fields = spread(rows9[...])
    y = iota((YE, NZ), 0)
    planes = []
    for da in range(3):
        lo, mid, hi = (fields[da * 3 + k : da * 3 + k + 1] for k in range(3))
        planes.append(jnp.where(y < T, lo, jnp.where(y < T + CY, mid, hi)))
    return planes, [plane_box(p) for p in planes]


def box_plane(boxes, x):
    lo, mid, hi = boxes
    if x <= -2:
        return 3.0 * lo
    if x == -1:
        return 2.0 * lo + mid
    if x == 0:
        return lo + 2.0 * mid
    if x < CX - 1:
        return 3.0 * mid
    if x == CX - 1:
        return 2.0 * mid + hi
    if x == CX:
        return mid + 2.0 * hi
    return 3.0 * hi


def kernel_pack_y(where, r, s, first, second, row):
    def copy(out, rows):
        out[0] = r[:, rows, :]
        out[1] = s[:, rows, :]

    @pl.when((where[1] & 1) == 0)
    def _():
        copy(first, slice(CY - T, CY))
        copy(second, slice(0, T))

    @pl.when((where[1] & 1) == 1)
    def _():
        copy(first, slice(0, T))
        copy(second, slice(CY - T, CY))

    def add(i, carry):
        ra, sa = carry
        for t in range(CY // T):
            ra = ra + r[i, tile(t)]
            sa = sa + s[i, tile(t)]
        return ra, sa

    zero = jnp.zeros((T, NZ), F32)
    ra, sa = lax.fori_loop(0, CX, add, (zero, zero))
    out = slab_sums(ra, 0) * (1.0 / CELLS) + slab_sums(sa, AGG)
    row[...] = jnp.broadcast_to(out, row.shape)


def kernel_pack_x(where, r, s, first, second, g, rown, sown, xfirst, xsecond, row, *, n_py):
    def sides(lo, hi):
        for k, (own, out) in enumerate(((r, rown), (s, sown))):
            out[:, :T] = lo[k]
            out[:, T : T + CY] = own[...]
            out[:, T + CY :] = hi[k]

    pl.when((where[1] & 1) == 0)(lambda: sides(second, first))
    pl.when((where[1] & 1) == 1)(lambda: sides(first, second))

    def faces(lo, hi):
        for k, own in enumerate((rown, sown)):
            lo[k] = own[:H]
            hi[k] = own[CX - H :]

    pl.when((where[0] & 1) == 0)(lambda: faces(xsecond, xfirst))
    pl.when((where[0] & 1) == 1)(lambda: faces(xfirst, xsecond))
    rows = g[...]
    for k in range(2):
        one = line_up(rows, k * AGG, n_py)
        row[:, k : k + 1, :] = jnp.broadcast_to(one[None], (row.shape[0], 1, row.shape[2]))


def smooth_last(rref, iref, zref, yref, n):
    def sweep(src, dst, i):
        for t, box, _ in neighbours(src, i, range(TILES)):
            dst[i, tile(t)] = (rref[i, tile(t)] + box) * iref[i, tile(t)]

    each(1, n - 1, lambda i: sweep(zref, yref, i))
    each(2, n - 2, lambda i: sweep(yref, zref, i))


def kernel_a(where, rown, sown, first, second, inverse, g1,
             rmid, smid, imid, v, u, row, rext, iext, zref, yref, *, n_px, n_py):
    a, b = where[0], where[1]
    y = iota((T, NZ), 0)

    def put(i, plane_of, inside):
        for t in range(TILES):
            rr, ss = plane_of(t)
            keep = inside
            if t == 0:
                keep = inside & (b > 0)
            if t == TILES - 1:
                keep = inside & (b < n_py - 1)
            inv = jnp.where(keep, 1.0 / (26.0 + ss), 0.0)
            rext[i, tile(t)] = rr
            iext[i, tile(t)] = inv
            zref[i, tile(t)] = rr * inv

    def mids(i, rr, ss):
        rmid[i - (H - V)] = rr
        smid[i - (H - V)] = ss

    def own(k):
        put(k + H, lambda t: (rown[k, tile(t)], sown[k, tile(t)]), a >= 0)
        mids(k + H, rown[k], sown[k])

    each(0, CX, own)

    def sides(lo, hi):
        each(0, H, lambda k: put(k, lambda t: (lo[0, k, tile(t)], lo[1, k, tile(t)]), a > 0))
        each(
            0, H,
            lambda k: put(
                k + H + CX, lambda t: (hi[0, k, tile(t)], hi[1, k, tile(t)]), a < n_px - 1
            ),
        )
        each(H - V, H, lambda k: mids(k, lo[0, k], lo[1, k]))
        each(0, V, lambda k: mids(k + H + CX, hi[0, k], hi[1, k]))

    pl.when((a & 1) == 0)(lambda: sides(second, first))
    pl.when((a & 1) == 1)(lambda: sides(first, second))
    smooth_last(rext, iext, zref, yref, XE)

    def apply(i, tiles):
        j = i - (H - V)
        for t, box, mid in neighbours(zref, i, tiles):
            v[j, tile(t)] = (26.0 + smid[j, tile(t)]) * mid - box
        imid[j] = iext[i]

    each(H - V, H, lambda i: apply(i, range(TILES)))
    each(H + CX, H + CX + V, lambda i: apply(i, range(TILES)))

    def apply_own(i, carry):
        ru, uv, av = carry
        j = i - (H - V)
        for t, box, mid in neighbours(zref, i, range(TILES)):
            vv = (26.0 + smid[j, tile(t)]) * mid - box
            v[j, tile(t)] = vv
            if 1 <= t < TILES - 1:
                u[i - H, tile(t - 1)] = mid
                ru = ru + fold(rext[i, tile(t)] * mid)
                uv = uv + fold(mid * vv)
                av = av + vv
        imid[j] = iext[i]
        return ru, uv, av

    zero = jnp.zeros((T, LANES), F32)
    ru, uv, av = lax.fori_loop(H, H + CX, apply_own, (zero, zero, jnp.zeros((T, NZ), F32)))
    m = g1[:, 0, :]
    lane = iota((1, LANES), 1)
    out = coarse_rows(inverse, m) + slab_sums(av, AGG) * (1.0 / CELLS)
    out = out + jnp.where(lane == 24, total(ru), 0.0) + jnp.where(lane == 25, total(uv), 0.0)
    row[...] = jnp.broadcast_to(out, row.shape)


def kernel_b(where, rmid, smid, imid, v, inverse, g1, g2,
             r1o, uo, vo, qo, row, scal, rref, qref, zref, yref, rows9, cref, *, n_px, n_py):
    g = g2[...]
    m, shifts = g1[:, 0, :], g1[:, 1, :]
    c = line_up(g, 0, n_py)
    w = line_up(g, AGG, n_py)
    lane = iota(g.shape, 1)
    tc = coarse_operator(c, shifts)
    rz = total(jnp.where(lane == 24, g, 0.0)) + CELLS * total(m * c)
    curv = total(jnp.where(lane == 25, g, 0.0)) + total(c * (2.0 * CELLS * w + tc))
    alpha = rz / curv
    e = w + tc * (1.0 / CELLS)
    mnew = m - alpha * e
    cnew = coarse_rows(inverse, mnew)
    planes, boxes = coarse_planes(where, g2, n_px, n_py, rows9)

    def image(i, pc, bc):
        for t in range(TILES):
            at = tile(t)
            q = v[i, at] + (27.0 + smid[i, at]) * pc[at] - bc[at]
            rr = rmid[i, at] - alpha * q
            qref[i, at] = q
            rref[i, at] = rr
            zref[i, at] = rr * imid[i, at]

    for i in (0, 1, 2, 3, XV - 4, XV - 3, XV - 2, XV - 1):
        block = 0 if i < V else 1 if i < V + CX else 2
        image(i, planes[block], box_plane(boxes, i - V))
    inner = 3.0 * boxes[1]
    each(V + 1, V + CX - 1, lambda i: image(i, planes[1], inner))
    smooth_last(rref, imid, zref, yref, XV)

    def apply(i, carry):
        ru, uv, uq, av = carry
        for t, box, uu in neighbours(zref, i, range(1, TILES - 1)):
            at, to = tile(t), tile(t - 1)
            vv = (26.0 + smid[i, at]) * uu - box
            rr, qq = rref[i, at], qref[i, at]
            uo[i - V, to] = uu
            vo[i - V, to] = vv
            r1o[i - V, to] = rr
            qo[i - V, to] = qq
            ru = ru + fold(rr * uu)
            uv = uv + fold(uu * vv)
            uq = uq + fold(uu * qq)
            av = av + vv
        return ru, uv, uq, av

    zero = jnp.zeros((T, LANES), F32)
    ru, uv, uq, av = lax.fori_loop(
        V, V + CX, apply, (zero, zero, zero, jnp.zeros((T, NZ), F32))
    )
    e_own = own_part(e, where, cref)
    m_own = own_part(mnew, where, cref)
    lane = iota((1, LANES), 1)
    out = cnew + slab_sums(av, AGG) * (1.0 / CELLS)
    out = out + jnp.where(lane == 24, total(ru) + CELLS * total(m_own * cnew), 0.0)
    out = out + jnp.where(lane == 25, total(uv), 0.0)
    out = out + jnp.where(lane == 26, total(uq) + CELLS * total(e_own * cnew), 0.0)
    row[...] = jnp.broadcast_to(out, row.shape)
    at = iota((8, LANES), 0)
    scal[...] = jnp.where(at == 0, rz, jnp.where(at == 1, curv, alpha))


def kernel_c(where, s, u, r1, un, vn, q, g1, g2, g3, scal, x, r2, rows9, *, n_px, n_py):
    g = g3[...]
    c = line_up(g, 0, n_py)
    w = line_up(g, AGG, n_py)
    lane = iota(g.shape, 1)
    tc = coarse_operator(c, g1[:, 1, :])
    rz, curv, alpha = scal[0:1, 0:1], scal[1:2, 0:1], scal[2:3, 0:1]
    rz1 = total(jnp.where(lane == 24, g, 0.0))
    zaz = total(jnp.where(lane == 25, g, 0.0)) + total(c * (2.0 * CELLS * w + tc))
    zq = total(jnp.where(lane == 26, g, 0.0))
    beta = rz1 / rz
    alpha2 = rz1 / (zaz + 2.0 * beta * zq + beta * beta * curv)
    first = alpha + alpha2 * beta
    planes, boxes = coarse_planes(where, g3, n_px, n_py, rows9)
    me = where[0] * n_py + where[1]
    c_old = spread(jnp.broadcast_to(g2[pl.ds(me, 1), :], (T, LANES)))
    rows = slice(T, T + CY)
    pc = planes[1][rows]
    base = first * c_old[0:1] + alpha2 * pc

    def finish(i, bc):
        for t in range(CY // T):
            at = tile(t)
            x[i, at] = first * u[i, at] + alpha2 * un[i, at] + base[at]
            image = vn[i, at] + (27.0 + s[i, at]) * pc[at] - bc[at] + beta * q[i, at]
            r2[i, at] = r1[i, at] - alpha2 * image

    for i in (0, CX - 1):
        finish(i, box_plane(boxes, i)[rows])
    inner = 3.0 * boxes[1][rows]
    each(1, CX - 1, lambda i: finish(i, inner))


VMEM = pl.BlockSpec(memory_space=pltpu.VMEM)
SMEM = pl.BlockSpec(memory_space=pltpu.SMEM)


def call(body, args, outs, scratch, name, **sizes):
    return pl.pallas_call(
        functools.partial(body, **sizes) if sizes else body,
        in_specs=[SMEM] + [VMEM] * (len(args) - 1),
        out_specs=[VMEM] * len(outs),
        out_shape=[jax.ShapeDtypeStruct(o, F32) for o in outs],
        scratch_shapes=[pltpu.VMEM(x, F32) for x in scratch],
        compiler_params=pltpu.CompilerParams(vmem_limit_bytes=32 * 1024 * 1024),
        name=name,
    )(*args)


def swap(x, axis, n, odd):
    pairs = [(i, i + 1) for i in range(odd, n - 1, 2)]
    return lax.ppermute(x, axis, pairs + [(j, i) for i, j in pairs])


def all_rows(x, axes):
    return lax.all_to_all(x, axes, 0, 0, tiled=True)


def per_device(right_side, shift, coarse_inverse, *, n_px, n_py):
    n = n_px * n_py
    width = n_py * AGG
    sizes = dict(n_px=n_px, n_py=n_py)
    where = jnp.stack([lax.axis_index("px"), lax.axis_index("py")]).astype(jnp.int32)
    face = (2, CX, T, NZ)
    first, second, row = call(
        kernel_pack_y, (where, right_side, shift), [face, face, (n_py, LANES)], [], "pack_y"
    )
    first = swap(first, "py", n_py, 0)
    second = swap(second, "py", n_py, 1)
    g = all_rows(row, "py")
    face = (2, H, YE, NZ)
    own = (CX, YE, NZ)
    rown, sown, first, second, row = call(
        kernel_pack_x, (where, right_side, shift, first, second, g),
        [own, own, face, face, (n_px, 2, width)], [], "pack_x", n_py=n_py,
    )
    first = swap(first, "px", n_px, 0)
    second = swap(second, "px", n_px, 1)
    g1 = all_rows(row, "px")
    rmid, smid, imid, v, u, row = call(
        kernel_a, (where, rown, sown, first, second, coarse_inverse, g1),
        [MID, MID, MID, MID, OWN, (n, LANES)], [EXT, EXT, EXT, EXT], "first", **sizes,
    )
    g2 = all_rows(row, ("px", "py"))
    r1, un, vn, q, row, scal = call(
        kernel_b, (where, rmid, smid, imid, v, coarse_inverse, g1, g2),
        [OWN, OWN, OWN, OWN, (n, LANES), (8, LANES)],
        [MID, MID, MID, MID, (16, LANES), (n_px, width)], "second", **sizes,
    )
    g3 = all_rows(row, ("px", "py"))
    return tuple(
        call(
            kernel_c, (where, shift, u, r1, un, vn, q, g1, g2, g3, scal),
            [OWN, OWN], [(16, LANES)], "third", **sizes,
        )
    )


def solution(mesh):
    placed = (P("px", "py", None), P("px", "py", None), P(("px", "py"), None))
    return jax.shard_map(
        functools.partial(per_device, n_px=mesh.shape["px"], n_py=mesh.shape["py"]),
        mesh=mesh,
        in_specs=placed,
        out_specs=(P("px", "py", None), P("px", "py", None)),
        check_vma=False,
    )
```

```python
import functools

import jax
import jax.numpy as jnp
from jax import lax
from jax.experimental import pallas as pl
from jax.experimental.pallas import tpu as pltpu
from jax.sharding import PartitionSpec as P

CX, CY, NZ = 16, 32, 512
AGG = 8
SLAB = NZ // AGG
CELLS = CX * CY * SLAB
H = 6
V = 3
T = 8
XE = CX + 2 * H
XV = CX + 2 * V
YE = CY + 2 * T
TILES = YE // T
LANES = 128
UNROLL = 8
PARTS = 4
F32 = jnp.float32
HIGH = lax.Precision.HIGHEST
OWN = (CX, CY, NZ)
EXT = (XE, YE, NZ)
MID = (XV, YE, NZ)


def tile(t):
    return slice(t * T, (t + 1) * T)


def iota(shape, axis):
    return lax.broadcasted_iota(jnp.int32, shape, axis)


def chunks(row):
    return [row[:, k * LANES : (k + 1) * LANES] for k in range(NZ // LANES)]


def lane_sum(rows):
    lane = iota((rows.shape[0], LANES), 1)
    parts = chunks(rows)
    up = [pltpu.roll(p, 1, axis=1) for p in parts]
    down = [pltpu.roll(p, LANES - 1, axis=1) for p in parts]
    zero = jnp.zeros_like(parts[0])
    out = []
    for k, p in enumerate(parts):
        left = jnp.where(lane == 0, up[k - 1] if k else zero, up[k])
        right = jnp.where(
            lane == LANES - 1, down[k + 1] if k + 1 < len(parts) else zero, down[k]
        )
        out.append(left + p + right)
    return jnp.concatenate(out, axis=1)


def tile_boxes(xsum, tiles):
    row = iota((T, NZ), 0)
    have = {}

    def get(t):
        if t not in have:
            x = xsum(t)
            have[t] = (x, pltpu.roll(x, 1, axis=0), pltpu.roll(x, T - 1, axis=0))
        return have[t]

    for t in tiles:
        x, up, down = get(t)
        if t > 0:
            up = jnp.where(row == 0, get(t - 1)[1], up)
        if t < TILES - 1:
            down = jnp.where(row == T - 1, get(t + 1)[2], down)
        yield t, lane_sum(up + x + down)


def neighbours(ref, i, tiles):
    def xsum(t):
        return ref[i - 1, tile(t)] + ref[i, tile(t)] + ref[i + 1, tile(t)]

    for t, box in tile_boxes(xsum, tiles):
        mid = ref[i, tile(t)]
        yield t, box - mid, mid


def plane_box(plane):
    parts = [box for _, box in tile_boxes(lambda t: plane[tile(t)], range(TILES))]
    return jnp.concatenate(parts, axis=0)


def each(low, high, body, unroll=UNROLL):
    def step(i, carry):
        body(i)
        return carry

    lax.fori_loop(low, high, step, 0, unroll=unroll)


def total(x):
    return jnp.sum(x, keepdims=True)


def fold(rows):
    a, b, c, d = chunks(rows)
    return (a + b) + (c + d)


def exact_dot(a, b):
    return jnp.dot(a, b, precision=HIGH, preferred_element_type=F32)


def slab_sums(acc, offset):
    cell, lane = iota((NZ, LANES), 0), iota((NZ, LANES), 1)
    pick = jnp.where(cell // SLAB + offset == lane, 1.0, 0.0).astype(F32)
    return jnp.sum(exact_dot(acc, pick), axis=0, keepdims=True)


def spread(rows):
    lane, cell = iota((LANES, NZ), 0), iota((LANES, NZ), 1)
    return exact_dot(rows, jnp.where(cell // SLAB == lane, 1.0, 0.0).astype(F32))


def line_up(rows, offset, n_py):
    width = n_py * AGG
    src, dst = iota((LANES, width), 0), iota((LANES, width), 1)
    repeat = jnp.where((dst & (AGG - 1)) + offset == src, 1.0, 0.0).astype(F32)
    wide = exact_dot(rows, repeat)
    row, lane = iota(wide.shape, 0), iota(wide.shape, 1)
    wide = jnp.where((row & (n_py - 1)) == lane // AGG, wide, 0.0)
    return jnp.sum(wide.reshape(rows.shape[0] // n_py, n_py, width), axis=1)


def coarse_rows(inverse, vector):
    n, width = vector.shape
    acc = jnp.zeros((AGG, width), F32)
    for k in range(n):
        acc = acc + inverse[:, k * width : (k + 1) * width] * vector[k : k + 1]
    column = jnp.sum(acc, axis=1, keepdims=True)
    row, lane = iota((AGG, LANES), 0), iota((AGG, LANES), 1)
    return jnp.sum(jnp.where(row == lane, column, 0.0), axis=0, keepdims=True)


def coarse_operator(c, shift_sums):
    n, width = c.shape
    row, lane = iota(c.shape, 0), iota(c.shape, 1)
    slab = lane & (AGG - 1)
    t = (
        (3.0 * SLAB - 2.0) * c
        + jnp.where(slab == 0, 0.0, pltpu.roll(c, 1, axis=1))
        + jnp.where(slab == AGG - 1, 0.0, pltpu.roll(c, width - 1, axis=1))
    )
    t = (
        (3.0 * CY - 2.0) * t
        + jnp.where(lane < AGG, 0.0, pltpu.roll(t, AGG, axis=1))
        + jnp.where(lane >= width - AGG, 0.0, pltpu.roll(t, width - AGG, axis=1))
    )
    t = (
        (3.0 * CX - 2.0) * t
        + jnp.where(row == 0, 0.0, pltpu.roll(t, 1, axis=0))
        + jnp.where(row == n - 1, 0.0, pltpu.roll(t, n - 1, axis=0))
    )
    return (27.0 * CELLS + shift_sums) * c - t


def own_part(vector, where, ref):
    ref[...] = vector
    mine = ref[pl.ds(where[0], 1), :]
    lane = iota(mine.shape, 1)
    mine = jnp.where(lane // AGG == where[1], mine, 0.0)
    src, dst = iota((mine.shape[1], LANES), 0), iota((mine.shape[1], LANES), 1)
    pick = jnp.where((src & (AGG - 1)) == dst, 1.0, 0.0).astype(F32)
    return exact_dot(jnp.broadcast_to(mine, (T, mine.shape[1])), pick)[:1]


def coarse_planes(where, gathered, n_px, n_py, rows9):
    a, b = where[0], where[1]
    rows9[...] = jnp.zeros_like(rows9)
    for da in (-1, 0, 1):
        for db in (-1, 0, 1):
            aa, bb = a + da, b + db
            inside = (aa >= 0) & (aa < n_px) & (bb >= 0) & (bb < n_py)
            k = jnp.clip(aa, 0, n_px - 1) * n_py + jnp.clip(bb, 0, n_py - 1)
            at = (da + 1) * 3 + db + 1
            rows9[at : at + 1] = jnp.where(inside, gathered[pl.ds(k, 1), :], 0.0)
    fields = spread(rows9[...])
    y = iota((YE, NZ), 0)
    planes = []
    for da in range(3):
        lo, mid, hi = (fields[da * 3 + k : da * 3 + k + 1] for k in range(3))
        planes.append(jnp.where(y < T, lo, jnp.where(y < T + CY, mid, hi)))
    return planes, [plane_box(p) for p in planes]


def box_plane(boxes, x):
    lo, mid, hi = boxes
    if x <= -2:
        return 3.0 * lo
    if x == -1:
        return 2.0 * lo + mid
    if x == 0:
        return lo + 2.0 * mid
    if x < CX - 1:
        return 3.0 * mid
    if x == CX - 1:
        return 2.0 * mid + hi
    if x == CX:
        return mid + 2.0 * hi
    return 3.0 * hi


class Field:
    def __init__(self, own, halo, width):
        self.own, self.halo, self.width = own, halo, width

    def __call__(self, i, t):
        outer = (self.halo.shape[0] - 2 * self.width) // 2
        if isinstance(i, int) and i < self.width:
            return self.halo[i + outer, tile(t)]
        if isinstance(i, int) and i >= self.width + CX:
            return self.halo[i + outer - CX, tile(t)]
        return self.own[i - self.width, tile(t)]


def over(low, high, width, body):
    for i in range(low, width):
        body(i)
    each(width, width + CX, body)
    for i in range(width + CX, high):
        body(i)


def kernel_pack_y(where, r_in, s_in, r, s, first, second, row, sems):
    size = CX // PARTS
    copies = [
        [
            pltpu.make_async_copy(
                src.at[pl.ds(k * size, size)], dst.at[pl.ds(k * size, size)], sems.at[f, k]
            )
            for k in range(PARTS)
        ]
        for f, (src, dst) in enumerate(((r_in, r), (s_in, s)))
    ]
    for group in copies:
        for copy in group:
            copy.start()
    even = (where[1] & 1) == 0
    sums = []
    for f, own in enumerate((r, s)):
        acc = jnp.zeros((T, NZ), F32)
        for k in range(PARTS):
            copies[f][k].wait()
            for i in range(k * size, (k + 1) * size):
                lo, hi = own[i, tile(0)], own[i, tile(CY // T - 1)]
                first[f, i] = jnp.where(even, hi, lo)
                second[f, i] = jnp.where(even, lo, hi)
                for t in range(CY // T):
                    acc = acc + own[i, tile(t)]
        sums.append(acc)
    out = slab_sums(sums[0], 0) * (1.0 / CELLS) + slab_sums(sums[1], AGG)
    row[...] = jnp.broadcast_to(out, row.shape)


def kernel_pack_x(where, r, s, first, second, g, rown, sown, xfirst, xsecond, row, *, n_py):
    even = (where[1] & 1) == 0
    for i in range(CX):
        for k, (own, out) in enumerate(((r, rown), (s, sown))):
            out[i, tile(0)] = jnp.where(even, second[k, i], first[k, i])
            out[i, tile(TILES - 1)] = jnp.where(even, first[k, i], second[k, i])
            for t in range(CY // T):
                out[i, tile(t + 1)] = own[i, tile(t)]
    even = (where[0] & 1) == 0

    def put(at, t, lo, hi):
        xfirst[at, tile(t)] = jnp.where(even, hi, lo)
        xsecond[at, tile(t)] = jnp.where(even, lo, hi)

    for t in range(TILES):
        for k in range(H - 1):
            put(k, t, rown[k, tile(t)], rown[CX - 1 - k, tile(t)])
            put(H - 1 + k, t, sown[k, tile(t)], sown[CX - 1 - k, tile(t)])
        lo, hi = (
            rown[i, tile(t)] / (26.0 + sown[i, tile(t)]) for i in (H - 1, CX - H)
        )
        put(2 * H - 2, t, lo, hi)
    rows = g[...]
    for k in range(2):
        one = line_up(rows, k * AGG, n_py)
        row[:, k : k + 1, :] = jnp.broadcast_to(one[None], (row.shape[0], 1, row.shape[2]))


def smooth_last(r, iref, zref, yref, n, width):
    def sweep(src, dst):
        def body(i):
            for t, box, _ in neighbours(src, i, range(TILES)):
                dst[i, tile(t)] = (r(i, t) + box) * iref[i, tile(t)]

        return body

    over(1, n - 1, width, sweep(zref, yref))
    over(2, n - 2, width, sweep(yref, zref))


def kernel_a(where, rown, sown, first, second, inverse, g1,
             rhalo, shalo, iext, v, zref, row, yref, *, n_px, n_py):
    a, b = where[0], where[1]
    even = (a & 1) == 0

    def invert(i, t, ss, inside):
        keep = inside
        if t == 0:
            keep = inside & (b > 0)
        if t == TILES - 1:
            keep = inside & (b < n_py - 1)
        inv = jnp.where(keep, 1.0 / (26.0 + ss), 0.0)
        iext[i, tile(t)] = inv
        return inv

    def own(i):
        for t in range(TILES):
            zref[i, tile(t)] = rown[i - H, tile(t)] * invert(i, t, sown[i - H, tile(t)], a >= 0)

    each(H, H + CX, own)
    for t in range(TILES):
        at = tile(t)

        def got(k):
            x, y = first[k, at], second[k, at]
            return jnp.where(even, y, x), jnp.where(even, x, y)

        for k in range(H - 1):
            for i, rr, ss, inside in zip(
                (H - 1 - k, H + CX + k), got(k), got(H - 1 + k), (a > 0, a < n_px - 1)
            ):
                at_halo = i if i < H else i - CX
                rhalo[at_halo, at] = rr
                shalo[at_halo, at] = ss
                zref[i, at] = rr * invert(i, t, ss, inside)
        zref[0, at], zref[XE - 1, at] = got(2 * H - 2)
    r, s = Field(rown, rhalo, H), Field(sown, shalo, H)
    smooth_last(r, iext, zref, yref, XE, H)

    def apply(i):
        for t, box, mid in neighbours(zref, i, range(TILES)):
            v[i - (H - V), tile(t)] = (26.0 + s(i, t)) * mid - box

    for i in (*range(H - V, H), *range(H + CX, H + CX + V)):
        apply(i)

    def apply_own(i, carry):
        ru, uv, av = carry
        for t, box, mid in neighbours(zref, i, range(TILES)):
            vv = (26.0 + s(i, t)) * mid - box
            v[i - (H - V), tile(t)] = vv
            if 1 <= t < TILES - 1:
                ru = ru + fold(r(i, t) * mid)
                uv = uv + fold(mid * vv)
                av = av + vv
        return ru, uv, av

    zero = jnp.zeros((T, LANES), F32)
    ru, uv, av = lax.fori_loop(
        H, H + CX, apply_own, (zero, zero, jnp.zeros((T, NZ), F32)), unroll=UNROLL
    )
    m = g1[:, 0, :]
    lane = iota((1, LANES), 1)
    out = coarse_rows(inverse, m) + slab_sums(av, AGG) * (1.0 / CELLS)
    out = out + jnp.where(lane == 24, total(ru), 0.0) + jnp.where(lane == 25, total(uv), 0.0)
    row[...] = jnp.broadcast_to(out, row.shape)


def kernel_b(where, rown, sown, rhalo, shalo, iext, v, inverse, g1, g2,
             rref, qref, zref, vo, row, scal, iref, yref, rows9, cref, *, n_px, n_py):
    g = g2[...]
    m, shifts = g1[:, 0, :], g1[:, 1, :]
    c = line_up(g, 0, n_py)
    w = line_up(g, AGG, n_py)
    lane = iota(g.shape, 1)
    tc = coarse_operator(c, shifts)
    rz = total(jnp.where(lane == 24, g, 0.0)) + CELLS * total(m * c)
    curv = total(jnp.where(lane == 25, g, 0.0)) + total(c * (2.0 * CELLS * w + tc))
    alpha = rz / curv
    e = w + tc * (1.0 / CELLS)
    mnew = m - alpha * e
    cnew = coarse_rows(inverse, mnew)
    planes, boxes = coarse_planes(where, g2, n_px, n_py, rows9)
    r, s = Field(rown, rhalo, V), Field(sown, shalo, V)

    def image(i, pc, bc):
        for t in range(TILES):
            at = tile(t)
            q = v[i, at] + (27.0 + s(i, t)) * pc[at] - bc[at]
            rr = r(i, t) - alpha * q
            inv = iext[i + (H - V), at]
            qref[i, at] = q
            rref[i, at] = rr
            zref[i, at] = rr * inv
            iref[i, at] = inv

    for i in (0, 1, 2, 3, XV - 4, XV - 3, XV - 2, XV - 1):
        block = 0 if i < V else 1 if i < V + CX else 2
        image(i, planes[block], box_plane(boxes, i - V))
    inner = 3.0 * boxes[1]
    each(V + 1, V + CX - 1, lambda i: image(i, planes[1], inner), unroll=2)
    smooth_last(lambda i, t: rref[i, tile(t)], iref, zref, yref, XV, V)

    def apply(i, carry):
        ru, uv, uq, av = carry
        for t, box, uu in neighbours(zref, i, range(1, TILES - 1)):
            at = tile(t)
            vv = (26.0 + s(i, t)) * uu - box
            vo[i - V, tile(t - 1)] = vv
            ru = ru + fold(rref[i, at] * uu)
            uv = uv + fold(uu * vv)
            uq = uq + fold(uu * qref[i, at])
            av = av + vv
        return ru, uv, uq, av

    zero = jnp.zeros((T, LANES), F32)
    ru, uv, uq, av = lax.fori_loop(
        V, V + CX, apply, (zero, zero, zero, jnp.zeros((T, NZ), F32)), unroll=UNROLL
    )
    e_own = own_part(e, where, cref)
    m_own = own_part(mnew, where, cref)
    lane = iota((1, LANES), 1)
    out = cnew + slab_sums(av, AGG) * (1.0 / CELLS)
    out = out + jnp.where(lane == 24, total(ru) + CELLS * total(m_own * cnew), 0.0)
    out = out + jnp.where(lane == 25, total(uv), 0.0)
    out = out + jnp.where(lane == 26, total(uq) + CELLS * total(e_own * cnew), 0.0)
    row[...] = jnp.broadcast_to(out, row.shape)
    at = iota((8, LANES), 0)
    scal[...] = jnp.where(at == 0, rz, jnp.where(at == 1, curv, alpha))


def kernel_c(where, sown, u, r1, un, vn, q, g1, g2, g3, scal, x_out, r_out,
             x, r2, rows9, sems, *, n_px, n_py):
    g = g3[...]
    c = line_up(g, 0, n_py)
    w = line_up(g, AGG, n_py)
    lane = iota(g.shape, 1)
    tc = coarse_operator(c, g1[:, 1, :])
    rz, curv, alpha = scal[0:1, 0:1], scal[1:2, 0:1], scal[2:3, 0:1]
    rz1 = total(jnp.where(lane == 24, g, 0.0))
    zaz = total(jnp.where(lane == 25, g, 0.0)) + total(c * (2.0 * CELLS * w + tc))
    zq = total(jnp.where(lane == 26, g, 0.0))
    beta = rz1 / rz
    alpha2 = rz1 / (zaz + 2.0 * beta * zq + beta * beta * curv)
    first = alpha + alpha2 * beta
    planes, boxes = coarse_planes(where, g3, n_px, n_py, rows9)
    me = where[0] * n_py + where[1]
    c_old = spread(jnp.broadcast_to(g2[pl.ds(me, 1), :], (T, LANES)))
    pc = planes[1][T : 2 * T]
    base = first * c_old + alpha2 * pc
    size = CX // PARTS
    copies = []
    for i in range(CX):
        bc = box_plane(boxes, i)
        for t in range(CY // T):
            to, at = tile(t), tile(t + 1)
            x[i, to] = first * u[i + H, at] + alpha2 * un[i + V, at] + base
            image = vn[i, to] + (27.0 + sown[i, at]) * pc - bc[at] + beta * q[i + V, at]
            r2[i, to] = r1[i + V, at] - alpha2 * image
        if (i + 1) % size == 0:
            k = i // size
            for f, (src, dst) in enumerate(((x, x_out), (r2, r_out))):
                part = pl.ds(k * size, size)
                copies.append(
                    pltpu.make_async_copy(src.at[part], dst.at[part], sems.at[f, k])
                )
                copies[-1].start()
    for copy in copies:
        copy.wait()


VMEM = pl.BlockSpec(memory_space=pltpu.VMEM)
SMEM = pl.BlockSpec(memory_space=pltpu.SMEM)
ANY = pl.BlockSpec(memory_space=pl.ANY)


def call(body, args, outs, scratch, name, in_specs=None, out_specs=None, **sizes):
    return pl.pallas_call(
        functools.partial(body, **sizes) if sizes else body,
        in_specs=in_specs or [SMEM] + [VMEM] * (len(args) - 1),
        out_specs=out_specs or [VMEM] * len(outs),
        out_shape=[jax.ShapeDtypeStruct(o, F32) for o in outs],
        scratch_shapes=[pltpu.VMEM(x, F32) if isinstance(x, tuple) else x for x in scratch],
        compiler_params=pltpu.CompilerParams(vmem_limit_bytes=32 * 1024 * 1024),
        name=name,
    )(*args)


def swap(x, axis, n, odd):
    pairs = [(i, i + 1) for i in range(odd, n - 1, 2)]
    return lax.ppermute(x, axis, pairs + [(j, i) for i, j in pairs])


def all_rows(x, axes):
    return lax.all_to_all(x, axes, 0, 0, tiled=True)


def per_device(right_side, shift, coarse_inverse, *, n_px, n_py):
    n = n_px * n_py
    width = n_py * AGG
    sizes = dict(n_px=n_px, n_py=n_py)
    copies = pltpu.SemaphoreType.DMA((2, PARTS))
    where = jnp.stack([lax.axis_index("px"), lax.axis_index("py")]).astype(jnp.int32)
    face = (2, CX, T, NZ)
    r, s, first, second, row = call(
        kernel_pack_y, (where, right_side, shift), [OWN, OWN, face, face, (n_py, LANES)],
        [copies], "pack_y", in_specs=[SMEM, ANY, ANY],
    )
    first = swap(first, "py", n_py, 0)
    second = swap(second, "py", n_py, 1)
    g = all_rows(row, "py")
    face = (2 * H - 1, YE, NZ)
    own = (CX, YE, NZ)
    rown, sown, first, second, row = call(
        kernel_pack_x, (where, r, s, first, second, g),
        [own, own, face, face, (n_px, 2, width)], [], "pack_x", n_py=n_py,
    )
    first = swap(first, "px", n_px, 0)
    second = swap(second, "px", n_px, 1)
    g1 = all_rows(row, "px")
    halo = (2 * H, YE, NZ)
    rhalo, shalo, iext, v, u, row = call(
        kernel_a, (where, rown, sown, first, second, coarse_inverse, g1),
        [halo, halo, EXT, MID, EXT, (n, LANES)], [EXT], "first", **sizes,
    )
    g2 = all_rows(row, ("px", "py"))
    r1, q, un, vn, row, scal = call(
        kernel_b, (where, rown, sown, rhalo, shalo, iext, v, coarse_inverse, g1, g2),
        [MID, MID, MID, OWN, (n, LANES), (8, LANES)],
        [MID, MID, (16, LANES), (n_px, width)], "second", **sizes,
    )
    g3 = all_rows(row, ("px", "py"))
    return tuple(
        call(
            kernel_c, (where, sown, u, r1, un, vn, q, g1, g2, g3, scal),
            [OWN, OWN], [OWN, OWN, (16, LANES), copies], "third",
            out_specs=[ANY, ANY], **sizes,
        )
    )


def solution(mesh):
    placed = (P("px", "py", None), P("px", "py", None), P(("px", "py"), None))
    return jax.shard_map(
        functools.partial(per_device, n_px=mesh.shape["px"], n_py=mesh.shape["py"]),
        mesh=mesh,
        in_specs=placed,
        out_specs=(P("px", "py", None), P("px", "py", None)),
        check_vma=False,
    )
```

```python
import functools

import jax
import jax.numpy as jnp
from jax import lax
from jax.experimental import pallas as pl
from jax.experimental.pallas import tpu as pltpu
from jax.sharding import PartitionSpec as P

CX, CY, NZ = 16, 32, 512
AGG = 8
SLAB = NZ // AGG
CELLS = CX * CY * SLAB
H = 3
T = 8
HY = 6
XE = CX + 2 * H
YE = CY + 2 * T
TILES = YE // T
LANES = 128
UNROLL = 8
PARTS = 4
F32 = jnp.float32
HIGH = lax.Precision.HIGHEST
OWN = (CX, CY, NZ)
EXT = (XE, YE, NZ)
TALL = (CX, YE, NZ)


def tile(t):
    return slice(t * T, (t + 1) * T)


def iota(shape, axis):
    return lax.broadcasted_iota(jnp.int32, shape, axis)


def chunks(row):
    return [row[:, k * LANES : (k + 1) * LANES] for k in range(NZ // LANES)]


def lane_sum(rows):
    lane = iota((rows.shape[0], LANES), 1)
    parts = chunks(rows)
    up = [pltpu.roll(p, 1, axis=1) for p in parts]
    down = [pltpu.roll(p, LANES - 1, axis=1) for p in parts]
    zero = jnp.zeros_like(parts[0])
    out = []
    for k, p in enumerate(parts):
        left = jnp.where(lane == 0, up[k - 1] if k else zero, up[k])
        right = jnp.where(
            lane == LANES - 1, down[k + 1] if k + 1 < len(parts) else zero, down[k]
        )
        out.append(left + p + right)
    return jnp.concatenate(out, axis=1)


def tile_boxes(xsum, tiles):
    row = iota((T, NZ), 0)
    have = {}

    def get(t):
        if t not in have:
            x = xsum(t)
            have[t] = (x, pltpu.roll(x, 1, axis=0), pltpu.roll(x, T - 1, axis=0))
        return have[t]

    for t in tiles:
        x, up, down = get(t)
        if t > 0:
            up = jnp.where(row == 0, get(t - 1)[1], up)
        if t < TILES - 1:
            down = jnp.where(row == T - 1, get(t + 1)[2], down)
        yield t, lane_sum(up + x + down)


def neighbours(ref, i, tiles):
    def xsum(t):
        return ref[i - 1, tile(t)] + ref[i, tile(t)] + ref[i + 1, tile(t)]

    for t, box in tile_boxes(xsum, tiles):
        mid = ref[i, tile(t)]
        yield t, box - mid, mid


def plane_box(plane):
    parts = [box for _, box in tile_boxes(lambda t: plane[tile(t)], range(TILES))]
    return jnp.concatenate(parts, axis=0)


def each(low, high, body, unroll=UNROLL):
    def step(i, carry):
        body(i)
        return carry

    lax.fori_loop(low, high, step, 0, unroll=unroll)


def total(x):
    return jnp.sum(x, keepdims=True)


def fold(rows):
    a, b, c, d = chunks(rows)
    return (a + b) + (c + d)


def exact_dot(a, b):
    return jnp.dot(a, b, precision=HIGH, preferred_element_type=F32)


def slab_sums(acc, offset):
    cell, lane = iota((NZ, LANES), 0), iota((NZ, LANES), 1)
    pick = jnp.where(cell // SLAB + offset == lane, 1.0, 0.0).astype(F32)
    return jnp.sum(exact_dot(acc, pick), axis=0, keepdims=True)


def spread(rows):
    lane, cell = iota((LANES, NZ), 0), iota((LANES, NZ), 1)
    return exact_dot(rows, jnp.where(cell // SLAB == lane, 1.0, 0.0).astype(F32))


def line_up(rows, offset, n_py):
    width = n_py * AGG
    src, dst = iota((LANES, width), 0), iota((LANES, width), 1)
    repeat = jnp.where((dst & (AGG - 1)) + offset == src, 1.0, 0.0).astype(F32)
    wide = exact_dot(rows, repeat)
    row, lane = iota(wide.shape, 0), iota(wide.shape, 1)
    wide = jnp.where((row & (n_py - 1)) == lane // AGG, wide, 0.0)
    return jnp.sum(wide.reshape(rows.shape[0] // n_py, n_py, width), axis=1)


def coarse_rows(inverse, vector):
    n, width = vector.shape
    acc = jnp.zeros((AGG, width), F32)
    for k in range(n):
        acc = acc + inverse[:, k * width : (k + 1) * width] * vector[k : k + 1]
    column = jnp.sum(acc, axis=1, keepdims=True)
    row, lane = iota((AGG, LANES), 0), iota((AGG, LANES), 1)
    return jnp.sum(jnp.where(row == lane, column, 0.0), axis=0, keepdims=True)


def coarse_operator(c, shift_sums):
    n, width = c.shape
    row, lane = iota(c.shape, 0), iota(c.shape, 1)
    slab = lane & (AGG - 1)
    t = (
        (3.0 * SLAB - 2.0) * c
        + jnp.where(slab == 0, 0.0, pltpu.roll(c, 1, axis=1))
        + jnp.where(slab == AGG - 1, 0.0, pltpu.roll(c, width - 1, axis=1))
    )
    t = (
        (3.0 * CY - 2.0) * t
        + jnp.where(lane < AGG, 0.0, pltpu.roll(t, AGG, axis=1))
        + jnp.where(lane >= width - AGG, 0.0, pltpu.roll(t, width - AGG, axis=1))
    )
    t = (
        (3.0 * CX - 2.0) * t
        + jnp.where(row == 0, 0.0, pltpu.roll(t, 1, axis=0))
        + jnp.where(row == n - 1, 0.0, pltpu.roll(t, n - 1, axis=0))
    )
    return (27.0 * CELLS + shift_sums) * c - t


def own_part(vector, where, ref):
    ref[...] = vector
    mine = ref[pl.ds(where[0], 1), :]
    lane = iota(mine.shape, 1)
    mine = jnp.where(lane // AGG == where[1], mine, 0.0)
    src, dst = iota((mine.shape[1], LANES), 0), iota((mine.shape[1], LANES), 1)
    pick = jnp.where((src & (AGG - 1)) == dst, 1.0, 0.0).astype(F32)
    return exact_dot(jnp.broadcast_to(mine, (T, mine.shape[1])), pick)[:1]


def coarse_planes(where, gathered, n_px, n_py, rows9):
    a, b = where[0], where[1]
    rows9[...] = jnp.zeros_like(rows9)
    for da in (-1, 0, 1):
        for db in (-1, 0, 1):
            aa, bb = a + da, b + db
            inside = (aa >= 0) & (aa < n_px) & (bb >= 0) & (bb < n_py)
            k = jnp.clip(aa, 0, n_px - 1) * n_py + jnp.clip(bb, 0, n_py - 1)
            at = (da + 1) * 3 + db + 1
            rows9[at : at + 1] = jnp.where(inside, gathered[pl.ds(k, 1), :], 0.0)
    fields = spread(rows9[...])
    y = iota((YE, NZ), 0)
    planes = []
    for da in range(3):
        lo, mid, hi = (fields[da * 3 + k : da * 3 + k + 1] for k in range(3))
        planes.append(jnp.where(y < T, lo, jnp.where(y < T + CY, mid, hi)))
    return planes, [plane_box(p) for p in planes]


def box_plane(boxes, x):
    lo, mid, hi = boxes
    if x <= -2:
        return 3.0 * lo
    if x == -1:
        return 2.0 * lo + mid
    if x == 0:
        return lo + 2.0 * mid
    if x < CX - 1:
        return 3.0 * mid
    if x == CX - 1:
        return 2.0 * mid + hi
    if x == CX:
        return mid + 2.0 * hi
    return 3.0 * hi


class Field:
    def __init__(self, own, halo):
        self.own, self.halo = own, halo

    def __call__(self, i, t):
        if isinstance(i, int) and i < H:
            return self.halo[i, tile(t)]
        if isinstance(i, int) and i >= H + CX:
            return self.halo[i - CX, tile(t)]
        return self.own[i - H, tile(t)]


def over(low, high, body):
    for i in range(low, H):
        body(i)
    each(H, H + CX, body)
    for i in range(H + CX, high):
        body(i)


def shifted(rows, k):
    return pltpu.roll(rows, k % T, axis=0) if k % T else rows


def squeeze(pieces, o):
    row = iota((T, NZ), 0)
    a, b, c, d = pieces
    return (
        jnp.where(row < 6, shifted(a, -o), shifted(b, 6 - o)),
        jnp.where(row < 4, shifted(b, -o - 2), shifted(c, 4 - o)),
        jnp.where(row < 2, shifted(c, -o - 4), shifted(d, 2 - o)),
    )


def unsqueeze(tiles, o):
    row = iota((T, NZ), 0)
    a, b, c = tiles
    return (
        shifted(a, o),
        jnp.where(row < o + 2, shifted(a, o - 6), shifted(b, o + 2)),
        jnp.where(row < o + 4, shifted(b, o - 4), shifted(c, o + 4)),
        shifted(c, o - 2),
    )


def kernel_pack_y(where, r_in, s_in, r, s, first, second, row, sems):
    size = CX // PARTS
    copies = [
        [
            pltpu.make_async_copy(
                src.at[pl.ds(k * size, size)], dst.at[pl.ds(k * size, size)], sems.at[f, k]
            )
            for k in range(PARTS)
        ]
        for f, (src, dst) in enumerate(((r_in, r), (s_in, s)))
    ]
    for group in copies:
        for copy in group:
            copy.start()
    even = (where[1] & 1) == 0
    sums = []
    for f, own in enumerate((r, s)):
        acc = jnp.zeros((T, NZ), F32)
        for k in range(PARTS):
            copies[f][k].wait()
            planes = range(k * size, (k + 1) * size)
            los = squeeze([own[i, tile(0)] for i in planes], 0)
            his = squeeze([own[i, tile(CY // T - 1)] for i in planes], T - HY)
            for j, (lo, hi) in enumerate(zip(los, his)):
                at = tile((f * PARTS + k) * 3 + j)
                first[at] = jnp.where(even, hi, lo)
                second[at] = jnp.where(even, lo, hi)
            for i in planes:
                for t in range(CY // T):
                    acc = acc + own[i, tile(t)]
        sums.append(acc)
    out = slab_sums(sums[0], 0) * (1.0 / CELLS) + slab_sums(sums[1], AGG)
    row[...] = jnp.broadcast_to(out, row.shape)


def kernel_pack_x(where, r, s, first, second, g, rown, sown, xfirst, xsecond, row, *, n_py):
    even = (where[1] & 1) == 0
    for f, (own, out) in enumerate(((r, rown), (s, sown))):
        for k in range(PARTS):
            ats = [tile((f * PARTS + k) * 3 + j) for j in range(3)]
            los = unsqueeze([jnp.where(even, second[at], first[at]) for at in ats], T - HY)
            his = unsqueeze([jnp.where(even, first[at], second[at]) for at in ats], 0)
            for j, (lo, hi) in enumerate(zip(los, his)):
                i = k * (CX // PARTS) + j
                out[i, tile(0)] = lo
                out[i, tile(TILES - 1)] = hi
                for t in range(CY // T):
                    out[i, tile(t + 1)] = own[i, tile(t)]
    even = (where[0] & 1) == 0
    for k in range(H):
        for at, own in ((k, rown), (H + k, sown)):
            for t in range(TILES):
                lo, hi = own[k, tile(t)], own[CX - 1 - k, tile(t)]
                xfirst[at, tile(t)] = jnp.where(even, hi, lo)
                xsecond[at, tile(t)] = jnp.where(even, lo, hi)
    rows = g[...]
    for k in range(2):
        one = line_up(rows, k * AGG, n_py)
        row[:, k : k + 1, :] = jnp.broadcast_to(one[None], (row.shape[0], 1, row.shape[2]))


def smooth_last(r, iref, zref, yref):
    def sweep(src, dst):
        def body(i):
            for t, box, _ in neighbours(src, i, range(TILES)):
                dst[i, tile(t)] = (r(i, t) + box) * iref[i, tile(t)]

        return body

    over(1, XE - 1, sweep(zref, yref))
    over(2, XE - 2, sweep(yref, zref))


def kernel_a(where, rown, sown, first, second, inverse, g1,
             rhalo, shalo, iext, v, zref, vfirst, vsecond, row, yref, *, n_px, n_py):
    a, b = where[0], where[1]
    even = (a & 1) == 0
    y = iota((T, NZ), 0)

    def start(i, t, rr, ss, inside):
        keep = inside
        if t == 0:
            keep = inside & (b > 0) & (y >= T - HY)
        if t == TILES - 1:
            keep = inside & (b < n_py - 1) & (y < HY)
        inv = jnp.where(keep, 1.0 / (26.0 + ss), 0.0)
        iext[i, tile(t)] = inv
        zref[i, tile(t)] = rr * inv

    def own(i):
        for t in range(TILES):
            start(i, t, rown[i - H, tile(t)], sown[i - H, tile(t)], a >= 0)

    each(H, H + CX, own)
    for t in range(TILES):
        at = tile(t)

        def got(k):
            x, z = first[k, at], second[k, at]
            return jnp.where(even, z, x), jnp.where(even, x, z)

        for k in range(H):
            for i, rr, ss, inside in zip(
                (H - 1 - k, H + CX + k), got(k), got(H + k), (a > 0, a < n_px - 1)
            ):
                at_halo = i if i < H else i - CX
                rhalo[at_halo, at] = rr
                shalo[at_halo, at] = ss
                start(i, t, rr, ss, inside)
    r, s = Field(rown, rhalo), Field(sown, shalo)
    smooth_last(r, iext, zref, yref)

    def apply(i, carry):
        ru, uv, av = carry
        for t, box, mid in neighbours(zref, i, range(TILES)):
            vv = (26.0 + s(i, t)) * mid - box
            v[i - H, tile(t)] = vv
            if 1 <= t < TILES - 1:
                ru = ru + fold(r(i, t) * mid)
                uv = uv + fold(mid * vv)
                av = av + vv
        return ru, uv, av

    zero = jnp.zeros((T, LANES), F32)
    ru, uv, av = lax.fori_loop(
        H, H + CX, apply, (zero, zero, jnp.zeros((T, NZ), F32)), unroll=UNROLL
    )
    for k in range(H):
        for t in range(TILES):
            lo, hi = v[k, tile(t)], v[CX - 1 - k, tile(t)]
            vfirst[k, tile(t)] = jnp.where(even, hi, lo)
            vsecond[k, tile(t)] = jnp.where(even, lo, hi)
    m = g1[:, 0, :]
    lane = iota((1, LANES), 1)
    out = coarse_rows(inverse, m) + slab_sums(av, AGG) * (1.0 / CELLS)
    out = out + jnp.where(lane == 24, total(ru), 0.0) + jnp.where(lane == 25, total(uv), 0.0)
    row[...] = jnp.broadcast_to(out, row.shape)


def kernel_b(where, rown, sown, rhalo, shalo, iext, vown, vfirst, vsecond, inverse, g1, g2,
             rref, qref, zref, vo, row, scal, yref, rows9, cref, *, n_px, n_py):
    g = g2[...]
    m, shifts = g1[:, 0, :], g1[:, 1, :]
    c = line_up(g, 0, n_py)
    w = line_up(g, AGG, n_py)
    lane = iota(g.shape, 1)
    tc = coarse_operator(c, shifts)
    rz = total(jnp.where(lane == 24, g, 0.0)) + CELLS * total(m * c)
    curv = total(jnp.where(lane == 25, g, 0.0)) + total(c * (2.0 * CELLS * w + tc))
    alpha = rz / curv
    e = w + tc * (1.0 / CELLS)
    mnew = m - alpha * e
    cnew = coarse_rows(inverse, mnew)
    planes, boxes = coarse_planes(where, g2, n_px, n_py, rows9)
    r, s = Field(rown, rhalo), Field(sown, shalo)
    even = (where[0] & 1) == 0

    def v(i, t):
        if isinstance(i, int) and not H <= i < H + CX:
            k = H - 1 - i if i < H else i - H - CX
            x, z = vfirst[k, tile(t)], vsecond[k, tile(t)]
            return jnp.where(even, z, x) if i < H else jnp.where(even, x, z)
        return vown[i - H, tile(t)]

    def image(i, pc, bc):
        for t in range(TILES):
            at = tile(t)
            q = v(i, t) + (27.0 + s(i, t)) * pc[at] - bc[at]
            rr = r(i, t) - alpha * q
            qref[i, at] = q
            rref[i, at] = rr
            zref[i, at] = rr * iext[i, at]

    for i in (*range(H + 1), *range(H + CX - 1, XE)):
        block = 0 if i < H else 1 if i < H + CX else 2
        image(i, planes[block], box_plane(boxes, i - H))
    inner = 3.0 * boxes[1]
    each(H + 1, H + CX - 1, lambda i: image(i, planes[1], inner), unroll=2)
    smooth_last(lambda i, t: rref[i, tile(t)], iext, zref, yref)

    def apply(i, carry):
        ru, uv, uq, av = carry
        for t, box, uu in neighbours(zref, i, range(1, TILES - 1)):
            at = tile(t)
            vv = (26.0 + s(i, t)) * uu - box
            vo[i - H, tile(t - 1)] = vv
            ru = ru + fold(rref[i, at] * uu)
            uv = uv + fold(uu * vv)
            uq = uq + fold(uu * qref[i, at])
            av = av + vv
        return ru, uv, uq, av

    zero = jnp.zeros((T, LANES), F32)
    ru, uv, uq, av = lax.fori_loop(
        H, H + CX, apply, (zero, zero, zero, jnp.zeros((T, NZ), F32)), unroll=UNROLL
    )
    e_own = own_part(e, where, cref)
    m_own = own_part(mnew, where, cref)
    lane = iota((1, LANES), 1)
    out = cnew + slab_sums(av, AGG) * (1.0 / CELLS)
    out = out + jnp.where(lane == 24, total(ru) + CELLS * total(m_own * cnew), 0.0)
    out = out + jnp.where(lane == 25, total(uv), 0.0)
    out = out + jnp.where(lane == 26, total(uq) + CELLS * total(e_own * cnew), 0.0)
    row[...] = jnp.broadcast_to(out, row.shape)
    at = iota((8, LANES), 0)
    scal[...] = jnp.where(at == 0, rz, jnp.where(at == 1, curv, alpha))


def kernel_c(where, sown, u, r1, un, vn, q, g1, g2, g3, scal, x_out, r_out,
             x, r2, rows9, sems, *, n_px, n_py):
    g = g3[...]
    c = line_up(g, 0, n_py)
    w = line_up(g, AGG, n_py)
    lane = iota(g.shape, 1)
    tc = coarse_operator(c, g1[:, 1, :])
    rz, curv, alpha = scal[0:1, 0:1], scal[1:2, 0:1], scal[2:3, 0:1]
    rz1 = total(jnp.where(lane == 24, g, 0.0))
    zaz = total(jnp.where(lane == 25, g, 0.0)) + total(c * (2.0 * CELLS * w + tc))
    zq = total(jnp.where(lane == 26, g, 0.0))
    beta = rz1 / rz
    alpha2 = rz1 / (zaz + 2.0 * beta * zq + beta * beta * curv)
    first = alpha + alpha2 * beta
    planes, boxes = coarse_planes(where, g3, n_px, n_py, rows9)
    me = where[0] * n_py + where[1]
    c_old = spread(jnp.broadcast_to(g2[pl.ds(me, 1), :], (T, LANES)))
    pc = planes[1][T : 2 * T]
    base = first * c_old + alpha2 * pc
    size = CX // PARTS
    copies = []
    for i in range(CX):
        bc = box_plane(boxes, i)
        for t in range(CY // T):
            to, at = tile(t), tile(t + 1)
            x[i, to] = first * u[i + H, at] + alpha2 * un[i + H, at] + base
            image = vn[i, to] + (27.0 + sown[i, at]) * pc - bc[at] + beta * q[i + H, at]
            r2[i, to] = r1[i + H, at] - alpha2 * image
        if (i + 1) % size == 0:
            k = i // size
            for f, (src, dst) in enumerate(((x, x_out), (r2, r_out))):
                part = pl.ds(k * size, size)
                copies.append(
                    pltpu.make_async_copy(src.at[part], dst.at[part], sems.at[f, k])
                )
                copies[-1].start()
    for copy in copies:
        copy.wait()


VMEM = pl.BlockSpec(memory_space=pltpu.VMEM)
SMEM = pl.BlockSpec(memory_space=pltpu.SMEM)
HBM = pl.BlockSpec(memory_space=pltpu.HBM)


def call(body, args, outs, scratch, name, in_specs=None, out_specs=None, **sizes):
    return pl.pallas_call(
        functools.partial(body, **sizes) if sizes else body,
        in_specs=in_specs or [SMEM] + [VMEM] * (len(args) - 1),
        out_specs=out_specs or [VMEM] * len(outs),
        out_shape=[jax.ShapeDtypeStruct(o, F32) for o in outs],
        scratch_shapes=[pltpu.VMEM(x, F32) if isinstance(x, tuple) else x for x in scratch],
        compiler_params=pltpu.CompilerParams(vmem_limit_bytes=32 * 1024 * 1024),
        name=name,
    )(*args)


def swap(x, axis, n, odd):
    pairs = [(i, i + 1) for i in range(odd, n - 1, 2)]
    return lax.ppermute(x, axis, pairs + [(j, i) for i, j in pairs])


def all_rows(x, axes):
    return lax.all_to_all(x, axes, 0, 0, tiled=True)


def per_device(right_side, shift, coarse_inverse, *, n_px, n_py):
    n = n_px * n_py
    width = n_py * AGG
    sizes = dict(n_px=n_px, n_py=n_py)
    copies = pltpu.SemaphoreType.DMA((2, PARTS))
    where = jnp.stack([lax.axis_index("px"), lax.axis_index("py")]).astype(jnp.int32)
    inputs = [pltpu.with_memory_space_constraint(f, pltpu.HBM) for f in (right_side, shift)]
    face = (2 * CX * HY, NZ)
    r, s, first, second, row = call(
        kernel_pack_y, (where, *inputs), [OWN, OWN, face, face, (n_py, LANES)],
        [copies], "pack_y", in_specs=[SMEM, HBM, HBM],
    )
    first = swap(first, "py", n_py, 0)
    second = swap(second, "py", n_py, 1)
    g = all_rows(row, "py")
    face = (2 * H, YE, NZ)
    rown, sown, first, second, row = call(
        kernel_pack_x, (where, r, s, first, second, g),
        [TALL, TALL, face, face, (n_px, 2, width)], [], "pack_x", n_py=n_py,
    )
    first = swap(first, "px", n_px, 0)
    second = swap(second, "px", n_px, 1)
    g1 = all_rows(row, "px")
    halo = (2 * H, YE, NZ)
    face = (H, YE, NZ)
    rhalo, shalo, iext, v, u, first, second, row = call(
        kernel_a, (where, rown, sown, first, second, coarse_inverse, g1),
        [halo, halo, EXT, TALL, EXT, face, face, (n, LANES)], [EXT], "first", **sizes,
    )
    first = swap(first, "px", n_px, 0)
    second = swap(second, "px", n_px, 1)
    g2 = all_rows(row, ("px", "py"))
    r1, q, un, vn, row, scal = call(
        kernel_b,
        (where, rown, sown, rhalo, shalo, iext, v, first, second, coarse_inverse, g1, g2),
        [EXT, EXT, EXT, OWN, (n, LANES), (8, LANES)],
        [EXT, (16, LANES), (n_px, width)], "second", **sizes,
    )
    g3 = all_rows(row, ("px", "py"))
    return tuple(
        call(
            kernel_c, (where, sown, u, r1, un, vn, q, g1, g2, g3, scal),
            [OWN, OWN], [OWN, OWN, (16, LANES), copies], "third",
            out_specs=[HBM, HBM], **sizes,
        )
    )


def solution(mesh):
    placed = (P("px", "py", None), P("px", "py", None), P(("px", "py"), None))
    return jax.shard_map(
        functools.partial(per_device, n_px=mesh.shape["px"], n_py=mesh.shape["py"]),
        mesh=mesh,
        in_specs=placed,
        out_specs=(P("px", "py", None), P("px", "py", None)),
        check_vma=False,
    )
```

```python
import functools

import jax
import jax.numpy as jnp
from jax import lax
from jax.experimental import pallas as pl
from jax.experimental.pallas import tpu as pltpu
from jax.sharding import PartitionSpec as P

CX, CY, NZ = 16, 32, 512
AGG = 8
SLAB = NZ // AGG
CELLS = CX * CY * SLAB
H = 3
T = 8
HY = 6
XE = CX + 2 * H
YE = CY + 2 * T
TILES = YE // T
LANES = 128
UNROLL = 8
PARTS = 4
F32 = jnp.float32
HIGH = lax.Precision.HIGHEST
OWN = (CX, CY, NZ)
EXT = (XE, YE, NZ)
TALL = (CX, YE, NZ)


def tile(t):
    return slice(t * T, (t + 1) * T)


def iota(shape, axis):
    return lax.broadcasted_iota(jnp.int32, shape, axis)


def chunks(row):
    return [row[:, k * LANES : (k + 1) * LANES] for k in range(NZ // LANES)]


def lane_sum(rows):
    lane = iota((rows.shape[0], LANES), 1)
    parts = chunks(rows)
    up = [pltpu.roll(p, 1, axis=1) for p in parts]
    down = [pltpu.roll(p, LANES - 1, axis=1) for p in parts]
    zero = jnp.zeros_like(parts[0])
    out = []
    for k, p in enumerate(parts):
        left = jnp.where(lane == 0, up[k - 1] if k else zero, up[k])
        right = jnp.where(
            lane == LANES - 1, down[k + 1] if k + 1 < len(parts) else zero, down[k]
        )
        out.append(left + p + right)
    return jnp.concatenate(out, axis=1)


def tile_boxes(xsum, tiles):
    row = iota((T, NZ), 0)
    have = {}

    def get(t):
        if t not in have:
            x = xsum(t)
            have[t] = (x, pltpu.roll(x, 1, axis=0), pltpu.roll(x, T - 1, axis=0))
        return have[t]

    for t in tiles:
        x, up, down = get(t)
        if t > 0:
            up = jnp.where(row == 0, get(t - 1)[1], up)
        if t < TILES - 1:
            down = jnp.where(row == T - 1, get(t + 1)[2], down)
        yield t, lane_sum(up + x + down)


def neighbours(ref, i, tiles):
    def xsum(t):
        return ref[i - 1, tile(t)] + ref[i, tile(t)] + ref[i + 1, tile(t)]

    for t, box in tile_boxes(xsum, tiles):
        mid = ref[i, tile(t)]
        yield t, box - mid, mid


def plane_box(plane):
    parts = [box for _, box in tile_boxes(lambda t: plane[tile(t)], range(TILES))]
    return jnp.concatenate(parts, axis=0)


def each(low, high, body, unroll=UNROLL):
    def step(i, carry):
        body(i)
        return carry

    lax.fori_loop(low, high, step, 0, unroll=unroll)


def total(x):
    return jnp.sum(x, keepdims=True)


def fold(rows):
    a, b, c, d = chunks(rows)
    return (a + b) + (c + d)


def exact_dot(a, b):
    return jnp.dot(a, b, precision=HIGH, preferred_element_type=F32)


def slab_sums(acc, offset):
    cell, lane = iota((NZ, LANES), 0), iota((NZ, LANES), 1)
    pick = jnp.where(cell // SLAB + offset == lane, 1.0, 0.0).astype(F32)
    return jnp.sum(exact_dot(acc, pick), axis=0, keepdims=True)


def spread(rows):
    lane, cell = iota((LANES, NZ), 0), iota((LANES, NZ), 1)
    return exact_dot(rows, jnp.where(cell // SLAB == lane, 1.0, 0.0).astype(F32))


def line_up(rows, offset, n_py):
    width = n_py * AGG
    src, dst = iota((LANES, width), 0), iota((LANES, width), 1)
    repeat = jnp.where((dst & (AGG - 1)) + offset == src, 1.0, 0.0).astype(F32)
    wide = exact_dot(rows, repeat)
    row, lane = iota(wide.shape, 0), iota(wide.shape, 1)
    wide = jnp.where((row & (n_py - 1)) == lane // AGG, wide, 0.0)
    return jnp.sum(wide.reshape(rows.shape[0] // n_py, n_py, width), axis=1)


def coarse_rows(inverse, vector):
    n, width = vector.shape
    acc = jnp.zeros((AGG, width), F32)
    for k in range(n):
        acc = acc + inverse[:, k * width : (k + 1) * width] * vector[k : k + 1]
    column = jnp.sum(acc, axis=1, keepdims=True)
    row, lane = iota((AGG, LANES), 0), iota((AGG, LANES), 1)
    return jnp.sum(jnp.where(row == lane, column, 0.0), axis=0, keepdims=True)


def coarse_operator(c, shift_sums):
    n, width = c.shape
    row, lane = iota(c.shape, 0), iota(c.shape, 1)
    slab = lane & (AGG - 1)
    t = (
        (3.0 * SLAB - 2.0) * c
        + jnp.where(slab == 0, 0.0, pltpu.roll(c, 1, axis=1))
        + jnp.where(slab == AGG - 1, 0.0, pltpu.roll(c, width - 1, axis=1))
    )
    t = (
        (3.0 * CY - 2.0) * t
        + jnp.where(lane < AGG, 0.0, pltpu.roll(t, AGG, axis=1))
        + jnp.where(lane >= width - AGG, 0.0, pltpu.roll(t, width - AGG, axis=1))
    )
    t = (
        (3.0 * CX - 2.0) * t
        + jnp.where(row == 0, 0.0, pltpu.roll(t, 1, axis=0))
        + jnp.where(row == n - 1, 0.0, pltpu.roll(t, n - 1, axis=0))
    )
    return (27.0 * CELLS + shift_sums) * c - t


def own_part(vector, where, ref):
    ref[...] = vector
    mine = ref[pl.ds(where[0], 1), :]
    lane = iota(mine.shape, 1)
    mine = jnp.where(lane // AGG == where[1], mine, 0.0)
    src, dst = iota((mine.shape[1], LANES), 0), iota((mine.shape[1], LANES), 1)
    pick = jnp.where((src & (AGG - 1)) == dst, 1.0, 0.0).astype(F32)
    return exact_dot(jnp.broadcast_to(mine, (T, mine.shape[1])), pick)[:1]


def coarse_planes(where, gathered, n_px, n_py, rows9):
    a, b = where[0], where[1]
    rows9[...] = jnp.zeros_like(rows9)
    for da in (-1, 0, 1):
        for db in (-1, 0, 1):
            aa, bb = a + da, b + db
            inside = (aa >= 0) & (aa < n_px) & (bb >= 0) & (bb < n_py)
            k = jnp.clip(aa, 0, n_px - 1) * n_py + jnp.clip(bb, 0, n_py - 1)
            at = (da + 1) * 3 + db + 1
            rows9[at : at + 1] = jnp.where(inside, gathered[pl.ds(k, 1), :], 0.0)
    fields = spread(rows9[...])
    y = iota((YE, NZ), 0)
    planes = []
    for da in range(3):
        lo, mid, hi = (fields[da * 3 + k : da * 3 + k + 1] for k in range(3))
        planes.append(jnp.where(y < T, lo, jnp.where(y < T + CY, mid, hi)))
    return planes, [plane_box(p) for p in planes]


def box_plane(boxes, x):
    lo, mid, hi = boxes
    if x <= -2:
        return 3.0 * lo
    if x == -1:
        return 2.0 * lo + mid
    if x == 0:
        return lo + 2.0 * mid
    if x < CX - 1:
        return 3.0 * mid
    if x == CX - 1:
        return 2.0 * mid + hi
    if x == CX:
        return mid + 2.0 * hi
    return 3.0 * hi


class Field:
    def __init__(self, own, halo):
        self.own, self.halo = own, halo

    def __call__(self, i, t):
        if isinstance(i, int) and i < H:
            return self.halo[i, tile(t)]
        if isinstance(i, int) and i >= H + CX:
            return self.halo[i - CX, tile(t)]
        return self.own[i - H, tile(t)]


def over(low, high, body):
    for i in range(low, H):
        body(i)
    each(H, H + CX, body)
    for i in range(H + CX, high):
        body(i)


def shifted(rows, k):
    return pltpu.roll(rows, k % T, axis=0) if k % T else rows


def squeeze(pieces, o):
    row = iota((T, NZ), 0)
    a, b, c, d = pieces
    return (
        jnp.where(row < 6, shifted(a, -o), shifted(b, 6 - o)),
        jnp.where(row < 4, shifted(b, -o - 2), shifted(c, 4 - o)),
        jnp.where(row < 2, shifted(c, -o - 4), shifted(d, 2 - o)),
    )


def unsqueeze(tiles, o):
    row = iota((T, NZ), 0)
    a, b, c = tiles
    return (
        shifted(a, o),
        jnp.where(row < o + 2, shifted(a, o - 6), shifted(b, o + 2)),
        jnp.where(row < o + 4, shifted(b, o - 4), shifted(c, o + 4)),
        shifted(c, o - 2),
    )


def kernel_pack_y(where, r_in, s_in, r, first, second, row, slo, shi, sems):
    size = CX // PARTS
    parts = [pl.ds(k * size, size) for k in range(PARTS)]
    r_copies = [
        pltpu.make_async_copy(r_in.at[p], r.at[p], sems.at[0, k]) for k, p in enumerate(parts)
    ]
    s_copies = [
        pltpu.make_async_copy(s_in.at[:, pl.ds(y, T)], out, sems.at[1, k])
        for k, (y, out) in enumerate(((0, slo), (CY - T, shi)))
    ]
    for copy in (*r_copies, *s_copies):
        copy.start()
    even = (where[1] & 1) == 0

    def pack(f, k, lo_of, hi_of):
        planes = range(k * size, (k + 1) * size)
        los = squeeze([lo_of(i) for i in planes], 0)
        his = squeeze([hi_of(i) for i in planes], T - HY)
        for j, (lo, hi) in enumerate(zip(los, his)):
            at = tile((f * PARTS + k) * 3 + j)
            first[at] = jnp.where(even, hi, lo)
            second[at] = jnp.where(even, lo, hi)

    acc = jnp.zeros((T, NZ), F32)
    for k in range(PARTS):
        r_copies[k].wait()
        pack(0, k, lambda i: r[i, tile(0)], lambda i: r[i, tile(CY // T - 1)])
        for i in range(k * size, (k + 1) * size):
            for t in range(CY // T):
                acc = acc + r[i, tile(t)]
    for copy in s_copies:
        copy.wait()
    for k in range(PARTS):
        pack(1, k, lambda i: slo[i], lambda i: shi[i])
    row[...] = jnp.broadcast_to(slab_sums(acc, 0) * (1.0 / CELLS), row.shape)


def kernel_pack_x(where, r, s, first, second, g, rown, sown, xfirst, xsecond, row, *, n_py):
    even = (where[1] & 1) == 0
    for f, (own, out) in enumerate(((r, rown), (s, sown))):
        for k in range(PARTS):
            ats = [tile((f * PARTS + k) * 3 + j) for j in range(3)]
            los = unsqueeze([jnp.where(even, second[at], first[at]) for at in ats], T - HY)
            his = unsqueeze([jnp.where(even, first[at], second[at]) for at in ats], 0)
            for j, (lo, hi) in enumerate(zip(los, his)):
                i = k * (CX // PARTS) + j
                out[i, tile(0)] = lo
                out[i, tile(TILES - 1)] = hi
                for t in range(CY // T):
                    out[i, tile(t + 1)] = own[i, tile(t)]
    even = (where[0] & 1) == 0
    for k in range(H):
        for at, own in ((k, rown), (H + k, sown)):
            for t in range(TILES):
                lo, hi = own[k, tile(t)], own[CX - 1 - k, tile(t)]
                xfirst[at, tile(t)] = jnp.where(even, hi, lo)
                xsecond[at, tile(t)] = jnp.where(even, lo, hi)
    row[...] = jnp.broadcast_to(line_up(g[...], 0, n_py), row.shape)


def smooth_last(r, iref, zref, yref):
    def sweep(src, dst):
        def body(i):
            for t, box, _ in neighbours(src, i, range(TILES)):
                dst[i, tile(t)] = (r(i, t) + box) * iref[i, tile(t)]

        return body

    over(1, XE - 1, sweep(zref, yref))
    over(2, XE - 2, sweep(yref, zref))


def kernel_a(where, rown, sown, first, second, inverse, g1,
             rhalo, shalo, iext, v, zref, vfirst, vsecond, row, yref, *, n_px, n_py):
    a, b = where[0], where[1]
    even = (a & 1) == 0
    y = iota((T, NZ), 0)

    def start(i, t, rr, ss, inside):
        keep = inside
        if t == 0:
            keep = inside & (b > 0) & (y >= T - HY)
        if t == TILES - 1:
            keep = inside & (b < n_py - 1) & (y < HY)
        inv = jnp.where(keep, 1.0 / (26.0 + ss), 0.0)
        iext[i, tile(t)] = inv
        zref[i, tile(t)] = rr * inv

    def own(i):
        for t in range(TILES):
            start(i, t, rown[i - H, tile(t)], sown[i - H, tile(t)], a >= 0)

    each(H, H + CX, own)
    for t in range(TILES):
        at = tile(t)

        def got(k):
            x, z = first[k, at], second[k, at]
            return jnp.where(even, z, x), jnp.where(even, x, z)

        for k in range(H):
            for i, rr, ss, inside in zip(
                (H - 1 - k, H + CX + k), got(k), got(H + k), (a > 0, a < n_px - 1)
            ):
                at_halo = i if i < H else i - CX
                rhalo[at_halo, at] = rr
                shalo[at_halo, at] = ss
                start(i, t, rr, ss, inside)
    r, s = Field(rown, rhalo), Field(sown, shalo)
    smooth_last(r, iext, zref, yref)

    def apply(i, carry):
        ru, uv, av, sa = carry
        for t, box, mid in neighbours(zref, i, range(TILES)):
            ss = s(i, t)
            vv = (26.0 + ss) * mid - box
            v[i - H, tile(t)] = vv
            if 1 <= t < TILES - 1:
                ru = ru + fold(r(i, t) * mid)
                uv = uv + fold(mid * vv)
                av = av + vv
                sa = sa + ss
        return ru, uv, av, sa

    zero = jnp.zeros((T, LANES), F32)
    wide = jnp.zeros((T, NZ), F32)
    ru, uv, av, sa = lax.fori_loop(H, H + CX, apply, (zero, zero, wide, wide), unroll=UNROLL)
    for k in range(H):
        for t in range(TILES):
            lo, hi = v[k, tile(t)], v[CX - 1 - k, tile(t)]
            vfirst[k, tile(t)] = jnp.where(even, hi, lo)
            vsecond[k, tile(t)] = jnp.where(even, lo, hi)
    lane = iota((1, LANES), 1)
    out = coarse_rows(inverse, g1[...]) + slab_sums(av, AGG) * (1.0 / CELLS)
    out = out + slab_sums(sa, 2 * AGG)
    out = out + jnp.where(lane == 24, total(ru), 0.0) + jnp.where(lane == 25, total(uv), 0.0)
    row[...] = jnp.broadcast_to(out, row.shape)


def kernel_b(where, rown, sown, rhalo, shalo, iext, vown, vfirst, vsecond, inverse, g1, g2,
             rref, qref, zref, vo, row, scal, shifts, yref, rows9, cref, *, n_px, n_py):
    g = g2[...]
    m = g1[...]
    c = line_up(g, 0, n_py)
    shifts[...] = line_up(g, 2 * AGG, n_py)
    w = line_up(g, AGG, n_py)
    lane = iota(g.shape, 1)
    tc = coarse_operator(c, shifts[...])
    rz = total(jnp.where(lane == 24, g, 0.0)) + CELLS * total(m * c)
    curv = total(jnp.where(lane == 25, g, 0.0)) + total(c * (2.0 * CELLS * w + tc))
    alpha = rz / curv
    e = w + tc * (1.0 / CELLS)
    mnew = m - alpha * e
    cnew = coarse_rows(inverse, mnew)
    planes, boxes = coarse_planes(where, g2, n_px, n_py, rows9)
    r, s = Field(rown, rhalo), Field(sown, shalo)
    even = (where[0] & 1) == 0

    def v(i, t):
        if isinstance(i, int) and not H <= i < H + CX:
            k = H - 1 - i if i < H else i - H - CX
            x, z = vfirst[k, tile(t)], vsecond[k, tile(t)]
            return jnp.where(even, z, x) if i < H else jnp.where(even, x, z)
        return vown[i - H, tile(t)]

    def image(i, pc, bc):
        for t in range(TILES):
            at = tile(t)
            q = v(i, t) + (27.0 + s(i, t)) * pc[at] - bc[at]
            rr = r(i, t) - alpha * q
            qref[i, at] = q
            rref[i, at] = rr
            zref[i, at] = rr * iext[i, at]

    for i in (*range(H + 1), *range(H + CX - 1, XE)):
        block = 0 if i < H else 1 if i < H + CX else 2
        image(i, planes[block], box_plane(boxes, i - H))
    inner = 3.0 * boxes[1]
    each(H + 1, H + CX - 1, lambda i: image(i, planes[1], inner), unroll=2)
    smooth_last(lambda i, t: rref[i, tile(t)], iext, zref, yref)

    def apply(i, carry):
        ru, uv, uq, av = carry
        for t, box, uu in neighbours(zref, i, range(1, TILES - 1)):
            at = tile(t)
            vv = (26.0 + s(i, t)) * uu - box
            vo[i - H, tile(t - 1)] = vv
            ru = ru + fold(rref[i, at] * uu)
            uv = uv + fold(uu * vv)
            uq = uq + fold(uu * qref[i, at])
            av = av + vv
        return ru, uv, uq, av

    zero = jnp.zeros((T, LANES), F32)
    ru, uv, uq, av = lax.fori_loop(
        H, H + CX, apply, (zero, zero, zero, jnp.zeros((T, NZ), F32)), unroll=UNROLL
    )
    e_own = own_part(e, where, cref)
    m_own = own_part(mnew, where, cref)
    lane = iota((1, LANES), 1)
    out = cnew + slab_sums(av, AGG) * (1.0 / CELLS)
    out = out + jnp.where(lane == 24, total(ru) + CELLS * total(m_own * cnew), 0.0)
    out = out + jnp.where(lane == 25, total(uv), 0.0)
    out = out + jnp.where(lane == 26, total(uq) + CELLS * total(e_own * cnew), 0.0)
    row[...] = jnp.broadcast_to(out, row.shape)
    at = iota((8, LANES), 0)
    scal[...] = jnp.where(at == 0, rz, jnp.where(at == 1, curv, alpha))


def kernel_c(where, sown, u, r1, un, vn, q, shifts, g2, g3, scal, x_out, r_out,
             x, r2, rows9, sems, *, n_px, n_py):
    g = g3[...]
    c = line_up(g, 0, n_py)
    w = line_up(g, AGG, n_py)
    lane = iota(g.shape, 1)
    tc = coarse_operator(c, shifts[...])
    rz, curv, alpha = scal[0:1, 0:1], scal[1:2, 0:1], scal[2:3, 0:1]
    rz1 = total(jnp.where(lane == 24, g, 0.0))
    zaz = total(jnp.where(lane == 25, g, 0.0)) + total(c * (2.0 * CELLS * w + tc))
    zq = total(jnp.where(lane == 26, g, 0.0))
    beta = rz1 / rz
    alpha2 = rz1 / (zaz + 2.0 * beta * zq + beta * beta * curv)
    first = alpha + alpha2 * beta
    planes, boxes = coarse_planes(where, g3, n_px, n_py, rows9)
    me = where[0] * n_py + where[1]
    c_old = spread(jnp.broadcast_to(g2[pl.ds(me, 1), :], (T, LANES)))
    pc = planes[1][T : 2 * T]
    base = first * c_old + alpha2 * pc
    size = CX // PARTS
    copies = []
    for i in range(CX):
        bc = box_plane(boxes, i)
        for t in range(CY // T):
            to, at = tile(t), tile(t + 1)
            x[i, to] = first * u[i + H, at] + alpha2 * un[i + H, at] + base
            image = vn[i, to] + (27.0 + sown[i, at]) * pc - bc[at] + beta * q[i + H, at]
            r2[i, to] = r1[i + H, at] - alpha2 * image
        if (i + 1) % size == 0:
            k = i // size
            for f, (src, dst) in enumerate(((x, x_out), (r2, r_out))):
                part = pl.ds(k * size, size)
                copies.append(
                    pltpu.make_async_copy(src.at[part], dst.at[part], sems.at[f, k])
                )
                copies[-1].start()
    for copy in copies:
        copy.wait()


VMEM = pl.BlockSpec(memory_space=pltpu.VMEM)
SMEM = pl.BlockSpec(memory_space=pltpu.SMEM)
HBM = pl.BlockSpec(memory_space=pltpu.HBM)


def call(body, args, outs, scratch, name, in_specs=None, out_specs=None, **sizes):
    return pl.pallas_call(
        functools.partial(body, **sizes) if sizes else body,
        in_specs=in_specs or [SMEM] + [VMEM] * (len(args) - 1),
        out_specs=out_specs or [VMEM] * len(outs),
        out_shape=[jax.ShapeDtypeStruct(o, F32) for o in outs],
        scratch_shapes=[pltpu.VMEM(x, F32) if isinstance(x, tuple) else x for x in scratch],
        compiler_params=pltpu.CompilerParams(vmem_limit_bytes=32 * 1024 * 1024),
        name=name,
    )(*args)


def swap(x, axis, n, odd):
    pairs = [(i, (i + 1) % n) for i in range(odd, n, 2)]
    return lax.ppermute(x, axis, pairs + [(j, i) for i, j in pairs])


def all_rows(x, axes):
    return lax.all_to_all(x, axes, 0, 0, tiled=True)


def per_device(right_side, shift, coarse_inverse, *, n_px, n_py):
    n = n_px * n_py
    width = n_py * AGG
    sizes = dict(n_px=n_px, n_py=n_py)
    copies = pltpu.SemaphoreType.DMA((2, PARTS))
    where = jnp.stack([lax.axis_index("px"), lax.axis_index("py")]).astype(jnp.int32)
    inputs = [pltpu.with_memory_space_constraint(f, pltpu.HBM) for f in (right_side, shift)]
    face = (2 * CX * HY, NZ)
    r, first, second, row = call(
        kernel_pack_y, (where, *inputs), [OWN, face, face, (n_py, LANES)],
        [(CX, T, NZ), (CX, T, NZ), copies], "pack_y", in_specs=[SMEM, HBM, HBM],
    )
    first = swap(first, "py", n_py, 0)
    second = swap(second, "py", n_py, 1)
    g = all_rows(row, "py")
    face = (2 * H, YE, NZ)
    rown, sown, first, second, row = call(
        kernel_pack_x, (where, r, shift, first, second, g),
        [TALL, TALL, face, face, (n_px, width)], [], "pack_x", n_py=n_py,
    )
    first = swap(first, "px", n_px, 0)
    second = swap(second, "px", n_px, 1)
    g1 = all_rows(row, "px")
    halo = (2 * H, YE, NZ)
    face = (H, YE, NZ)
    rhalo, shalo, iext, v, u, first, second, row = call(
        kernel_a, (where, rown, sown, first, second, coarse_inverse, g1),
        [halo, halo, EXT, TALL, EXT, face, face, (n, LANES)], [EXT], "first", **sizes,
    )
    first = swap(first, "px", n_px, 0)
    second = swap(second, "px", n_px, 1)
    g2 = all_rows(row, ("px", "py"))
    r1, q, un, vn, row, scal, shifts = call(
        kernel_b,
        (where, rown, sown, rhalo, shalo, iext, v, first, second, coarse_inverse, g1, g2),
        [EXT, EXT, EXT, OWN, (n, LANES), (8, LANES), (n_px, width)],
        [EXT, (16, LANES), (n_px, width)], "second", **sizes,
    )
    g3 = all_rows(row, ("px", "py"))
    return tuple(
        call(
            kernel_c, (where, sown, u, r1, un, vn, q, shifts, g2, g3, scal),
            [OWN, OWN], [OWN, OWN, (16, LANES), copies], "third",
            out_specs=[HBM, HBM], **sizes,
        )
    )


def solution(mesh):
    placed = (P("px", "py", None), P("px", "py", None), P(("px", "py"), None))
    return jax.shard_map(
        functools.partial(per_device, n_px=mesh.shape["px"], n_py=mesh.shape["py"]),
        mesh=mesh,
        in_specs=placed,
        out_specs=(P("px", "py", None), P("px", "py", None)),
        check_vma=False,
    )
```

```python
import functools

import jax
import jax.numpy as jnp
from jax import lax
from jax.experimental import pallas as pl
from jax.experimental.pallas import tpu as pltpu
from jax.sharding import PartitionSpec as P

CX, CY, NZ = 16, 32, 512
AGG = 8
SLAB = NZ // AGG
CELLS = CX * CY * SLAB
H = 3
T = 8
HY = 6
XE = CX + 2 * H
YE = CY + 2 * T
TILES = YE // T
LANES = 128
UNROLL = 8
PARTS = 4
F32 = jnp.float32
OWN = (CX, CY, NZ)
EXT = (XE, YE, NZ)
TALL = (CX, YE, NZ)


def tile(t):
    return slice(t * T, (t + 1) * T)


def iota(shape, axis):
    return lax.broadcasted_iota(jnp.int32, shape, axis)


def chunks(row):
    return [row[:, k * LANES : (k + 1) * LANES] for k in range(NZ // LANES)]


def lane_sum(rows):
    lane = iota((rows.shape[0], LANES), 1)
    parts = chunks(rows)
    up = [pltpu.roll(p, 1, axis=1) for p in parts]
    down = [pltpu.roll(p, LANES - 1, axis=1) for p in parts]
    zero = jnp.zeros_like(parts[0])
    out = []
    for k, p in enumerate(parts):
        left = jnp.where(lane == 0, up[k - 1] if k else zero, up[k])
        right = jnp.where(
            lane == LANES - 1, down[k + 1] if k + 1 < len(parts) else zero, down[k]
        )
        out.append(left + p + right)
    return jnp.concatenate(out, axis=1)


def tile_boxes(xsum, tiles):
    row = iota((T, NZ), 0)
    have = {}

    def get(t):
        if t not in have:
            x = xsum(t)
            have[t] = (x, pltpu.roll(x, 1, axis=0), pltpu.roll(x, T - 1, axis=0))
        return have[t]

    for t in tiles:
        x, up, down = get(t)
        if t > 0:
            up = jnp.where(row == 0, get(t - 1)[1], up)
        if t < TILES - 1:
            down = jnp.where(row == T - 1, get(t + 1)[2], down)
        yield t, lane_sum(up + x + down)


def neighbours(ref, i, tiles):
    def xsum(t):
        return ref[i - 1, tile(t)] + ref[i, tile(t)] + ref[i + 1, tile(t)]

    for t, box in tile_boxes(xsum, tiles):
        mid = ref[i, tile(t)]
        yield t, box - mid, mid


def plane_box(plane):
    parts = [box for _, box in tile_boxes(lambda t: plane[tile(t)], range(TILES))]
    return jnp.concatenate(parts, axis=0)


def each(low, high, body, unroll=UNROLL):
    def step(i, carry):
        body(i)
        return carry

    lax.fori_loop(low, high, step, 0, unroll=unroll)


def total(x):
    return jnp.sum(x, keepdims=True)


def fold(rows):
    a, b, c, d = chunks(rows)
    return (a + b) + (c + d)


def slab_sums(acc, offset):
    lane = iota((T, LANES), 1)
    out = jnp.zeros((T, LANES), F32)
    for k, part in enumerate(chunks(acc)):
        for h, half in enumerate((lane < SLAB, lane >= SLAB)):
            one = jnp.sum(jnp.where(half, part, 0.0), axis=1, keepdims=True)
            out = jnp.where(lane == offset + 2 * k + h, one, out)
    return jnp.sum(out, axis=0, keepdims=True)


def spread(rows):
    low = iota((rows.shape[0], LANES), 1) < SLAB
    return jnp.concatenate(
        [jnp.where(low, rows[:, j : j + 1], rows[:, j + 1 : j + 2]) for j in range(0, AGG, 2)],
        axis=1,
    )


def line_up(rows, offset, n_py):
    lane = iota(rows.shape, 1)
    rows = jnp.where((lane >= offset) & (lane < offset + AGG), rows, 0.0)
    if offset:
        rows = pltpu.roll(rows, LANES - offset, axis=1)
    out = []
    for k in range(rows.shape[0] // n_py):
        part = rows[k * n_py : (k + 1) * n_py]
        part = pltpu.roll(part, 0, axis=1, stride=AGG, stride_axis=0)
        out.append(jnp.sum(part, axis=0, keepdims=True)[:, : n_py * AGG])
    return jnp.concatenate(out, axis=0)


def coarse_rows(inverse, vector):
    n, width = vector.shape
    acc = jnp.zeros((AGG, width), F32)
    for k in range(n):
        acc = acc + inverse[:, k * width : (k + 1) * width] * vector[k : k + 1]
    column = jnp.sum(acc, axis=1, keepdims=True)
    row, lane = iota((AGG, LANES), 0), iota((AGG, LANES), 1)
    return jnp.sum(jnp.where(row == lane, column, 0.0), axis=0, keepdims=True)


def coarse_operator(c, shift_sums):
    n, width = c.shape
    row, lane = iota(c.shape, 0), iota(c.shape, 1)
    slab = lane & (AGG - 1)
    t = (
        (3.0 * SLAB - 2.0) * c
        + jnp.where(slab == 0, 0.0, pltpu.roll(c, 1, axis=1))
        + jnp.where(slab == AGG - 1, 0.0, pltpu.roll(c, width - 1, axis=1))
    )
    t = (
        (3.0 * CY - 2.0) * t
        + jnp.where(lane < AGG, 0.0, pltpu.roll(t, AGG, axis=1))
        + jnp.where(lane >= width - AGG, 0.0, pltpu.roll(t, width - AGG, axis=1))
    )
    t = (
        (3.0 * CX - 2.0) * t
        + jnp.where(row == 0, 0.0, pltpu.roll(t, 1, axis=0))
        + jnp.where(row == n - 1, 0.0, pltpu.roll(t, n - 1, axis=0))
    )
    return (27.0 * CELLS + shift_sums) * c - t


def coarse_planes(where, gathered, n_px, n_py, rows9):
    a, b = where[0], where[1]
    rows9[...] = jnp.zeros_like(rows9)
    for da in (-1, 0, 1):
        for db in (-1, 0, 1):
            aa, bb = a + da, b + db
            inside = (aa >= 0) & (aa < n_px) & (bb >= 0) & (bb < n_py)
            k = jnp.clip(aa, 0, n_px - 1) * n_py + jnp.clip(bb, 0, n_py - 1)
            at = (da + 1) * 3 + db + 1
            rows9[at : at + 1] = jnp.where(inside, gathered[pl.ds(k, 1), :], 0.0)
    fields = spread(rows9[...])
    y = iota((YE, NZ), 0)
    planes = []
    for da in range(3):
        lo, mid, hi = (fields[da * 3 + k : da * 3 + k + 1] for k in range(3))
        planes.append(jnp.where(y < T, lo, jnp.where(y < T + CY, mid, hi)))
    return planes, [plane_box(p) for p in planes]


def box_plane(boxes, x):
    lo, mid, hi = boxes
    if x <= -2:
        return 3.0 * lo
    if x == -1:
        return 2.0 * lo + mid
    if x == 0:
        return lo + 2.0 * mid
    if x < CX - 1:
        return 3.0 * mid
    if x == CX - 1:
        return 2.0 * mid + hi
    if x == CX:
        return mid + 2.0 * hi
    return 3.0 * hi


class Field:
    def __init__(self, own, halo):
        self.own, self.halo = own, halo

    def __call__(self, i, t):
        if isinstance(i, int) and i < H:
            return self.halo[i, tile(t)]
        if isinstance(i, int) and i >= H + CX:
            return self.halo[i - CX, tile(t)]
        return self.own[i - H, tile(t)]


def over(low, high, body):
    for i in range(low, H):
        body(i)
    each(H, H + CX, body)
    for i in range(H + CX, high):
        body(i)


def shifted(rows, k):
    return pltpu.roll(rows, k % T, axis=0) if k % T else rows


def squeeze(pieces, o):
    row = iota((T, NZ), 0)
    a, b, c, d = pieces
    return (
        jnp.where(row < 6, shifted(a, -o), shifted(b, 6 - o)),
        jnp.where(row < 4, shifted(b, -o - 2), shifted(c, 4 - o)),
        jnp.where(row < 2, shifted(c, -o - 4), shifted(d, 2 - o)),
    )


def unsqueeze(tiles, o):
    row = iota((T, NZ), 0)
    a, b, c = tiles
    return (
        shifted(a, o),
        jnp.where(row < o + 2, shifted(a, o - 6), shifted(b, o + 2)),
        jnp.where(row < o + 4, shifted(b, o - 4), shifted(c, o + 4)),
        shifted(c, o - 2),
    )


def kernel_pack_y(where, r_in, s_in, r, first, second, row, slo, shi, sems):
    size = CX // PARTS
    parts = [pl.ds(k * size, size) for k in range(PARTS)]
    r_copies = [
        pltpu.make_async_copy(r_in.at[p], r.at[p], sems.at[0, k]) for k, p in enumerate(parts)
    ]
    s_copies = [
        pltpu.make_async_copy(s_in.at[:, pl.ds(y, T)], out, sems.at[1, k])
        for k, (y, out) in enumerate(((0, slo), (CY - T, shi)))
    ]
    for copy in (*r_copies, *s_copies):
        copy.start()
    even = (where[1] & 1) == 0

    def pack(f, k, lo_of, hi_of):
        planes = range(k * size, (k + 1) * size)
        los = squeeze([lo_of(i) for i in planes], 0)
        his = squeeze([hi_of(i) for i in planes], T - HY)
        for j, (lo, hi) in enumerate(zip(los, his)):
            at = tile((f * PARTS + k) * 3 + j)
            first[at] = jnp.where(even, hi, lo)
            second[at] = jnp.where(even, lo, hi)

    acc = jnp.zeros((T, NZ), F32)
    for k in range(PARTS):
        r_copies[k].wait()
        pack(0, k, lambda i: r[i, tile(0)], lambda i: r[i, tile(CY // T - 1)])
        for i in range(k * size, (k + 1) * size):
            for t in range(CY // T):
                acc = acc + r[i, tile(t)]
    for copy in s_copies:
        copy.wait()
    for k in range(PARTS):
        pack(1, k, lambda i: slo[i], lambda i: shi[i])
    row[...] = jnp.broadcast_to(slab_sums(acc, 0) * (1.0 / CELLS), row.shape)


def kernel_pack_x(where, r, s, first, second, g, rown, sown, xfirst, xsecond, row, *, n_py):
    even = (where[1] & 1) == 0
    for f, (own, out) in enumerate(((r, rown), (s, sown))):
        for k in range(PARTS):
            ats = [tile((f * PARTS + k) * 3 + j) for j in range(3)]
            los = unsqueeze([jnp.where(even, second[at], first[at]) for at in ats], T - HY)
            his = unsqueeze([jnp.where(even, first[at], second[at]) for at in ats], 0)
            for j, (lo, hi) in enumerate(zip(los, his)):
                i = k * (CX // PARTS) + j
                out[i, tile(0)] = lo
                out[i, tile(TILES - 1)] = hi
                for t in range(CY // T):
                    out[i, tile(t + 1)] = own[i, tile(t)]
    even = (where[0] & 1) == 0
    for k in range(H):
        for at, own in ((k, rown), (H + k, sown)):
            for t in range(TILES):
                lo, hi = own[k, tile(t)], own[CX - 1 - k, tile(t)]
                xfirst[at, tile(t)] = jnp.where(even, hi, lo)
                xsecond[at, tile(t)] = jnp.where(even, lo, hi)
    row[...] = jnp.broadcast_to(line_up(g[...], 0, n_py), row.shape)


def smooth_last(r, iref, zref, yref):
    def sweep(src, dst):
        def body(i):
            for t, box, _ in neighbours(src, i, range(TILES)):
                dst[i, tile(t)] = (r(i, t) + box) * iref[i, tile(t)]

        return body

    over(1, XE - 1, sweep(zref, yref))
    over(2, XE - 2, sweep(yref, zref))


def kernel_a(where, rown, sown, first, second, inverse, g1,
             rhalo, shalo, iext, v, zref, vfirst, vsecond, row, yref, *, n_px, n_py):
    a, b = where[0], where[1]
    even = (a & 1) == 0
    y = iota((T, NZ), 0)

    def start(i, t, rr, ss, inside):
        keep = inside
        if t == 0:
            keep = inside & (b > 0) & (y >= T - HY)
        if t == TILES - 1:
            keep = inside & (b < n_py - 1) & (y < HY)
        inv = jnp.where(keep, 1.0 / (26.0 + ss), 0.0)
        iext[i, tile(t)] = inv
        zref[i, tile(t)] = rr * inv

    def own(i):
        for t in range(TILES):
            start(i, t, rown[i - H, tile(t)], sown[i - H, tile(t)], a >= 0)

    each(H, H + CX, own)
    for t in range(TILES):
        at = tile(t)

        def got(k):
            x, z = first[k, at], second[k, at]
            return jnp.where(even, z, x), jnp.where(even, x, z)

        for k in range(H):
            for i, rr, ss, inside in zip(
                (H - 1 - k, H + CX + k), got(k), got(H + k), (a > 0, a < n_px - 1)
            ):
                at_halo = i if i < H else i - CX
                rhalo[at_halo, at] = rr
                shalo[at_halo, at] = ss
                start(i, t, rr, ss, inside)
    r, s = Field(rown, rhalo), Field(sown, shalo)
    smooth_last(r, iext, zref, yref)

    def apply(i, carry):
        ru, uv, av, sa = carry
        for t, box, mid in neighbours(zref, i, range(TILES)):
            ss = s(i, t)
            vv = (26.0 + ss) * mid - box
            v[i - H, tile(t)] = vv
            if 1 <= t < TILES - 1:
                ru = ru + fold(r(i, t) * mid)
                uv = uv + fold(mid * vv)
                av = av + vv
                sa = sa + ss
        return ru, uv, av, sa

    zero = jnp.zeros((T, LANES), F32)
    wide = jnp.zeros((T, NZ), F32)
    ru, uv, av, sa = lax.fori_loop(H, H + CX, apply, (zero, zero, wide, wide), unroll=UNROLL)
    for k in range(H):
        for t in range(TILES):
            lo, hi = v[k, tile(t)], v[CX - 1 - k, tile(t)]
            vfirst[k, tile(t)] = jnp.where(even, hi, lo)
            vsecond[k, tile(t)] = jnp.where(even, lo, hi)
    lane = iota((1, LANES), 1)
    out = coarse_rows(inverse, g1[...]) + slab_sums(av, AGG) * (1.0 / CELLS)
    out = out + slab_sums(sa, 2 * AGG)
    out = out + jnp.where(lane == 24, total(ru), 0.0) + jnp.where(lane == 25, total(uv), 0.0)
    row[...] = jnp.broadcast_to(out, row.shape)


def kernel_b(where, rown, sown, rhalo, shalo, iext, vown, vfirst, vsecond, inverse, g1, g2,
             rref, qref, zref, vo, row, scal, coarse, yref, rows9, *, n_px, n_py):
    g = g2[...]
    m = g1[...]
    c = line_up(g, 0, n_py)
    shifts = line_up(g, 2 * AGG, n_py)
    w = line_up(g, AGG, n_py)
    lane = iota(g.shape, 1)
    tc = coarse_operator(c, shifts)
    rz = total(jnp.where(lane == 24, g, 0.0)) + CELLS * total(m * c)
    curv = total(jnp.where(lane == 25, g, 0.0)) + total(c * (2.0 * CELLS * w + tc))
    alpha = rz / curv
    e = w + tc * (1.0 / CELLS)
    mnew = m - alpha * e
    coarse[0], coarse[1], coarse[2] = shifts, mnew, e
    cnew = coarse_rows(inverse, mnew)
    planes, boxes = coarse_planes(where, g2, n_px, n_py, rows9)
    r, s = Field(rown, rhalo), Field(sown, shalo)
    even = (where[0] & 1) == 0

    def v(i, t):
        if isinstance(i, int) and not H <= i < H + CX:
            k = H - 1 - i if i < H else i - H - CX
            x, z = vfirst[k, tile(t)], vsecond[k, tile(t)]
            return jnp.where(even, z, x) if i < H else jnp.where(even, x, z)
        return vown[i - H, tile(t)]

    def image(i, pc, bc):
        for t in range(TILES):
            at = tile(t)
            q = v(i, t) + (27.0 + s(i, t)) * pc[at] - bc[at]
            rr = r(i, t) - alpha * q
            qref[i, at] = q
            rref[i, at] = rr
            zref[i, at] = rr * iext[i, at]

    for i in (*range(H + 1), *range(H + CX - 1, XE)):
        block = 0 if i < H else 1 if i < H + CX else 2
        image(i, planes[block], box_plane(boxes, i - H))
    inner = 3.0 * boxes[1]
    each(H + 1, H + CX - 1, lambda i: image(i, planes[1], inner), unroll=2)
    smooth_last(lambda i, t: rref[i, tile(t)], iext, zref, yref)

    def apply(i, carry):
        ru, uv, uq, av = carry
        for t, box, uu in neighbours(zref, i, range(1, TILES - 1)):
            at = tile(t)
            vv = (26.0 + s(i, t)) * uu - box
            vo[i - H, tile(t - 1)] = vv
            ru = ru + fold(rref[i, at] * uu)
            uv = uv + fold(uu * vv)
            uq = uq + fold(uu * qref[i, at])
            av = av + vv
        return ru, uv, uq, av

    zero = jnp.zeros((T, LANES), F32)
    ru, uv, uq, av = lax.fori_loop(
        H, H + CX, apply, (zero, zero, zero, jnp.zeros((T, NZ), F32)), unroll=UNROLL
    )
    lane = iota((1, LANES), 1)
    out = cnew + slab_sums(av, AGG) * (1.0 / CELLS)
    for k, part in ((24, ru), (25, uv), (26, uq)):
        out = out + jnp.where(lane == k, total(part), 0.0)
    row[...] = jnp.broadcast_to(out, row.shape)
    at = iota((8, LANES), 0)
    scal[...] = jnp.where(at == 0, rz, jnp.where(at == 1, curv, alpha))


def kernel_c(where, sown, u, r1, un, vn, q, coarse, g2, g3, scal, x_out, r_out,
             x, r2, rows9, sems, *, n_px, n_py):
    g = g3[...]
    c = line_up(g, 0, n_py)
    w = line_up(g, AGG, n_py)
    lane = iota(g.shape, 1)
    tc = coarse_operator(c, coarse[0])
    rz, curv, alpha = scal[0:1, 0:1], scal[1:2, 0:1], scal[2:3, 0:1]
    rz1 = total(jnp.where(lane == 24, g, 0.0)) + CELLS * total(c * coarse[1])
    zaz = total(jnp.where(lane == 25, g, 0.0)) + total(c * (2.0 * CELLS * w + tc))
    zq = total(jnp.where(lane == 26, g, 0.0)) + CELLS * total(c * coarse[2])
    beta = rz1 / rz
    alpha2 = rz1 / (zaz + 2.0 * beta * zq + beta * beta * curv)
    first = alpha + alpha2 * beta
    planes, boxes = coarse_planes(where, g3, n_px, n_py, rows9)
    me = where[0] * n_py + where[1]
    c_old = spread(jnp.broadcast_to(g2[pl.ds(me, 1), :], (T, LANES)))
    pc = planes[1][T : 2 * T]
    base = first * c_old + alpha2 * pc
    size = CX // PARTS
    copies = []
    for i in range(CX):
        bc = box_plane(boxes, i)
        for t in range(CY // T):
            to, at = tile(t), tile(t + 1)
            x[i, to] = first * u[i + H, at] + alpha2 * un[i + H, at] + base
            image = vn[i, to] + (27.0 + sown[i, at]) * pc - bc[at] + beta * q[i + H, at]
            r2[i, to] = r1[i + H, at] - alpha2 * image
        if (i + 1) % size == 0:
            k = i // size
            for f, (src, dst) in enumerate(((x, x_out), (r2, r_out))):
                part = pl.ds(k * size, size)
                copies.append(
                    pltpu.make_async_copy(src.at[part], dst.at[part], sems.at[f, k])
                )
                copies[-1].start()
    for copy in copies:
        copy.wait()


VMEM = pl.BlockSpec(memory_space=pltpu.VMEM)
SMEM = pl.BlockSpec(memory_space=pltpu.SMEM)
HBM = pl.BlockSpec(memory_space=pltpu.HBM)


def call(body, args, outs, scratch, name, in_specs=None, out_specs=None, **sizes):
    return pl.pallas_call(
        functools.partial(body, **sizes) if sizes else body,
        in_specs=in_specs or [SMEM] + [VMEM] * (len(args) - 1),
        out_specs=out_specs or [VMEM] * len(outs),
        out_shape=[jax.ShapeDtypeStruct(o, F32) for o in outs],
        scratch_shapes=[pltpu.VMEM(x, F32) if isinstance(x, tuple) else x for x in scratch],
        compiler_params=pltpu.CompilerParams(vmem_limit_bytes=32 * 1024 * 1024),
        name=name,
    )(*args)


def swap(x, axis, n, odd):
    pairs = [(i, (i + 1) % n) for i in range(odd, n, 2)]
    return lax.ppermute(x, axis, pairs + [(j, i) for i, j in pairs])


def all_rows(x, axes):
    return lax.all_to_all(x, axes, 0, 0, tiled=True)


def per_device(right_side, shift, coarse_inverse, *, n_px, n_py):
    n = n_px * n_py
    width = n_py * AGG
    sizes = dict(n_px=n_px, n_py=n_py)
    copies = pltpu.SemaphoreType.DMA((2, PARTS))
    where = jnp.stack([lax.axis_index("px"), lax.axis_index("py")]).astype(jnp.int32)
    inputs = [pltpu.with_memory_space_constraint(f, pltpu.HBM) for f in (right_side, shift)]
    face = (2 * CX * HY, NZ)
    r, first, second, row = call(
        kernel_pack_y, (where, *inputs), [OWN, face, face, (n_py, LANES)],
        [(CX, T, NZ), (CX, T, NZ), copies], "pack_y", in_specs=[SMEM, HBM, HBM],
    )
    first = swap(first, "py", n_py, 0)
    second = swap(second, "py", n_py, 1)
    g = all_rows(row, "py")
    face = (2 * H, YE, NZ)
    rown, sown, first, second, row = call(
        kernel_pack_x, (where, r, shift, first, second, g),
        [TALL, TALL, face, face, (n_px, width)], [], "pack_x", n_py=n_py,
    )
    first = swap(first, "px", n_px, 0)
    second = swap(second, "px", n_px, 1)
    g1 = all_rows(row, "px")
    halo = (2 * H, YE, NZ)
    face = (H, YE, NZ)
    rhalo, shalo, iext, v, u, first, second, row = call(
        kernel_a, (where, rown, sown, first, second, coarse_inverse, g1),
        [halo, halo, EXT, TALL, EXT, face, face, (n, LANES)], [EXT], "first", **sizes,
    )
    first = swap(first, "px", n_px, 0)
    second = swap(second, "px", n_px, 1)
    g2 = all_rows(row, ("px", "py"))
    r1, q, un, vn, row, scal, coarse = call(
        kernel_b,
        (where, rown, sown, rhalo, shalo, iext, v, first, second, coarse_inverse, g1, g2),
        [EXT, EXT, EXT, OWN, (n, LANES), (8, LANES), (3, n_px, width)],
        [EXT, (16, LANES)], "second", **sizes,
    )
    g3 = all_rows(row, ("px", "py"))
    return tuple(
        call(
            kernel_c, (where, sown, u, r1, un, vn, q, coarse, g2, g3, scal),
            [OWN, OWN], [OWN, OWN, (16, LANES), copies], "third",
            out_specs=[HBM, HBM], **sizes,
        )
    )


def solution(mesh):
    placed = (P("px", "py", None), P("px", "py", None), P(("px", "py"), None))
    return jax.shard_map(
        functools.partial(per_device, n_px=mesh.shape["px"], n_py=mesh.shape["py"]),
        mesh=mesh,
        in_specs=placed,
        out_specs=(P("px", "py", None), P("px", "py", None)),
        check_vma=False,
    )
```

```python
import functools

import jax
import jax.numpy as jnp
from jax import lax
from jax.experimental import pallas as pl
from jax.experimental.pallas import tpu as pltpu
from jax.sharding import PartitionSpec as P

CX, CY, NZ = 16, 32, 512
AGG = 8
SLAB = NZ // AGG
CELLS = CX * CY * SLAB
H = 3
T = 8
HY = 6
XE = CX + 2 * H
YE = CY + 2 * T
TILES = YE // T
LANES = 128
UNROLL = 16
PARTS = 4
F32 = jnp.float32
OWN = (CX, CY, NZ)
EXT = (XE, YE, NZ)
TALL = (CX, YE, NZ)


def tile(t):
    return slice(t * T, (t + 1) * T)


def iota(shape, axis):
    return lax.broadcasted_iota(jnp.int32, shape, axis)


def chunks(row):
    return [row[:, k * LANES : (k + 1) * LANES] for k in range(NZ // LANES)]


def lane_sum(rows):
    lane = iota((rows.shape[0], LANES), 1)
    parts = chunks(rows)
    up = [pltpu.roll(p, 1, axis=1) for p in parts]
    down = [pltpu.roll(p, LANES - 1, axis=1) for p in parts]
    zero = jnp.zeros_like(parts[0])
    out = []
    for k, p in enumerate(parts):
        left = jnp.where(lane == 0, up[k - 1] if k else zero, up[k])
        right = jnp.where(
            lane == LANES - 1, down[k + 1] if k + 1 < len(parts) else zero, down[k]
        )
        out.append(left + p + right)
    return jnp.concatenate(out, axis=1)


def tile_boxes(xsum, tiles):
    row = iota((T, NZ), 0)
    have = {}

    def get(t):
        if t not in have:
            x = xsum(t)
            have[t] = (x, pltpu.roll(x, 1, axis=0), pltpu.roll(x, T - 1, axis=0))
        return have[t]

    for t in tiles:
        x, up, down = get(t)
        if t > 0:
            up = jnp.where(row == 0, get(t - 1)[1], up)
        if t < TILES - 1:
            down = jnp.where(row == T - 1, get(t + 1)[2], down)
        yield t, lane_sum(up + x + down)


def neighbours(ref, i, tiles):
    def xsum(t):
        return ref[i - 1, tile(t)] + ref[i, tile(t)] + ref[i + 1, tile(t)]

    for t, box in tile_boxes(xsum, tiles):
        mid = ref[i, tile(t)]
        yield t, box - mid, mid


def plane_box(plane):
    parts = [box for _, box in tile_boxes(lambda t: plane[tile(t)], range(TILES))]
    return jnp.concatenate(parts, axis=0)


def each(low, high, body, unroll=UNROLL):
    def step(i, carry):
        body(i)
        return carry

    lax.fori_loop(low, high, step, 0, unroll=unroll)


def total(x):
    return jnp.sum(x, keepdims=True)


def fold(rows):
    a, b, c, d = chunks(rows)
    return (a + b) + (c + d)


def slab_sums(acc, offset):
    lane = iota((T, LANES), 1)
    out = jnp.zeros((T, LANES), F32)
    for k, part in enumerate(chunks(acc)):
        for h, half in enumerate((lane < SLAB, lane >= SLAB)):
            one = jnp.sum(jnp.where(half, part, 0.0), axis=1, keepdims=True)
            out = jnp.where(lane == offset + 2 * k + h, one, out)
    return jnp.sum(out, axis=0, keepdims=True)


def spread(rows):
    low = iota((rows.shape[0], LANES), 1) < SLAB
    return jnp.concatenate(
        [jnp.where(low, rows[:, j : j + 1], rows[:, j + 1 : j + 2]) for j in range(0, AGG, 2)],
        axis=1,
    )


def line_up(rows, offset, n_py):
    lane = iota(rows.shape, 1)
    rows = jnp.where((lane >= offset) & (lane < offset + AGG), rows, 0.0)
    if offset:
        rows = pltpu.roll(rows, LANES - offset, axis=1)
    out = []
    for k in range(rows.shape[0] // n_py):
        part = rows[k * n_py : (k + 1) * n_py]
        part = pltpu.roll(part, 0, axis=1, stride=AGG, stride_axis=0)
        out.append(jnp.sum(part, axis=0, keepdims=True)[:, : n_py * AGG])
    return jnp.concatenate(out, axis=0)


def coarse_rows(inverse, vector):
    n, width = vector.shape
    acc = jnp.zeros((AGG, width), F32)
    for k in range(n):
        acc = acc + inverse[:, k * width : (k + 1) * width] * vector[k : k + 1]
    column = jnp.sum(acc, axis=1, keepdims=True)
    row, lane = iota((AGG, LANES), 0), iota((AGG, LANES), 1)
    return jnp.sum(jnp.where(row == lane, column, 0.0), axis=0, keepdims=True)


def coarse_operator(c, shift_sums):
    n, width = c.shape
    row, lane = iota(c.shape, 0), iota(c.shape, 1)
    slab = lane & (AGG - 1)
    t = (
        (3.0 * SLAB - 2.0) * c
        + jnp.where(slab == 0, 0.0, pltpu.roll(c, 1, axis=1))
        + jnp.where(slab == AGG - 1, 0.0, pltpu.roll(c, width - 1, axis=1))
    )
    t = (
        (3.0 * CY - 2.0) * t
        + jnp.where(lane < AGG, 0.0, pltpu.roll(t, AGG, axis=1))
        + jnp.where(lane >= width - AGG, 0.0, pltpu.roll(t, width - AGG, axis=1))
    )
    t = (
        (3.0 * CX - 2.0) * t
        + jnp.where(row == 0, 0.0, pltpu.roll(t, 1, axis=0))
        + jnp.where(row == n - 1, 0.0, pltpu.roll(t, n - 1, axis=0))
    )
    return (27.0 * CELLS + shift_sums) * c - t


def coarse_planes(where, gathered, n_px, n_py, rows9):
    a, b = where[0], where[1]
    rows9[...] = jnp.zeros_like(rows9)
    for da in (-1, 0, 1):
        for db in (-1, 0, 1):
            aa, bb = a + da, b + db
            inside = (aa >= 0) & (aa < n_px) & (bb >= 0) & (bb < n_py)
            k = jnp.clip(aa, 0, n_px - 1) * n_py + jnp.clip(bb, 0, n_py - 1)
            at = (da + 1) * 3 + db + 1
            rows9[at : at + 1] = jnp.where(inside, gathered[pl.ds(k, 1), :], 0.0)
    fields = spread(rows9[...])
    y = iota((YE, NZ), 0)
    planes = []
    for da in range(3):
        lo, mid, hi = (fields[da * 3 + k : da * 3 + k + 1] for k in range(3))
        planes.append(jnp.where(y < T, lo, jnp.where(y < T + CY, mid, hi)))
    return planes, [plane_box(p) for p in planes]


def box_plane(boxes, x):
    lo, mid, hi = boxes
    if x <= -2:
        return 3.0 * lo
    if x == -1:
        return 2.0 * lo + mid
    if x == 0:
        return lo + 2.0 * mid
    if x < CX - 1:
        return 3.0 * mid
    if x == CX - 1:
        return 2.0 * mid + hi
    if x == CX:
        return mid + 2.0 * hi
    return 3.0 * hi


class Field:
    def __init__(self, own, halo):
        self.own, self.halo = own, halo

    def __call__(self, i, t):
        if isinstance(i, int) and i < H:
            return self.halo[i, tile(t)]
        if isinstance(i, int) and i >= H + CX:
            return self.halo[i - CX, tile(t)]
        return self.own[i - H, tile(t)]


def over(low, high, body):
    for i in range(low, H):
        body(i)
    each(H, H + CX, body)
    for i in range(H + CX, high):
        body(i)


def shifted(rows, k):
    return pltpu.roll(rows, k % T, axis=0) if k % T else rows


def squeeze(pieces, o):
    row = iota((T, NZ), 0)
    a, b, c, d = pieces
    return (
        jnp.where(row < 6, shifted(a, -o), shifted(b, 6 - o)),
        jnp.where(row < 4, shifted(b, -o - 2), shifted(c, 4 - o)),
        jnp.where(row < 2, shifted(c, -o - 4), shifted(d, 2 - o)),
    )


def unsqueeze(tiles, o):
    row = iota((T, NZ), 0)
    a, b, c = tiles
    return (
        shifted(a, o),
        jnp.where(row < o + 2, shifted(a, o - 6), shifted(b, o + 2)),
        jnp.where(row < o + 4, shifted(b, o - 4), shifted(c, o + 4)),
        shifted(c, o - 2),
    )


def kernel_pack_y(where, r_in, s_in, r, first, second, row, slo, shi, sems):
    size = CX // PARTS
    parts = [pl.ds(k * size, size) for k in range(PARTS)]
    r_copies = [
        pltpu.make_async_copy(r_in.at[p], r.at[p], sems.at[0, k]) for k, p in enumerate(parts)
    ]
    s_copies = [
        pltpu.make_async_copy(s_in.at[:, pl.ds(y, T)], out, sems.at[1, k])
        for k, (y, out) in enumerate(((0, slo), (CY - T, shi)))
    ]
    for copy in (*r_copies, *s_copies):
        copy.start()
    even = (where[1] & 1) == 0

    def pack(f, k, lo_of, hi_of):
        planes = range(k * size, (k + 1) * size)
        los = squeeze([lo_of(i) for i in planes], 0)
        his = squeeze([hi_of(i) for i in planes], T - HY)
        for j, (lo, hi) in enumerate(zip(los, his)):
            at = tile((f * PARTS + k) * 3 + j)
            first[at] = jnp.where(even, hi, lo)
            second[at] = jnp.where(even, lo, hi)

    acc = jnp.zeros((T, NZ), F32)
    for k in range(PARTS):
        r_copies[k].wait()
        pack(0, k, lambda i: r[i, tile(0)], lambda i: r[i, tile(CY // T - 1)])
        for i in range(k * size, (k + 1) * size):
            for t in range(CY // T):
                acc = acc + r[i, tile(t)]
    for copy in s_copies:
        copy.wait()
    for k in range(PARTS):
        pack(1, k, lambda i: slo[i], lambda i: shi[i])
    row[...] = jnp.broadcast_to(slab_sums(acc, 0) * (1.0 / CELLS), row.shape)


def kernel_pack_x(where, r, s, first, second, g, rown, sown, xfirst, xsecond, row, *, n_py):
    even = (where[1] & 1) == 0
    for f, (own, out) in enumerate(((r, rown), (s, sown))):
        for k in range(PARTS):
            ats = [tile((f * PARTS + k) * 3 + j) for j in range(3)]
            los = unsqueeze([jnp.where(even, second[at], first[at]) for at in ats], T - HY)
            his = unsqueeze([jnp.where(even, first[at], second[at]) for at in ats], 0)
            for j, (lo, hi) in enumerate(zip(los, his)):
                i = k * (CX // PARTS) + j
                out[i, tile(0)] = lo
                out[i, tile(TILES - 1)] = hi
                for t in range(CY // T):
                    out[i, tile(t + 1)] = own[i, tile(t)]
    even = (where[0] & 1) == 0
    for k in range(H):
        for at, own in ((k, rown), (H + k, sown)):
            for t in range(TILES):
                lo, hi = own[k, tile(t)], own[CX - 1 - k, tile(t)]
                xfirst[at, tile(t)] = jnp.where(even, hi, lo)
                xsecond[at, tile(t)] = jnp.where(even, lo, hi)
    row[...] = jnp.broadcast_to(line_up(g[...], 0, n_py), row.shape)


def smooth_last(r, iref, zref, yref):
    def sweep(src, dst):
        def body(i):
            for t, box, _ in neighbours(src, i, range(TILES)):
                dst[i, tile(t)] = (r(i, t) + box) * iref[i, tile(t)]

        return body

    over(1, XE - 1, sweep(zref, yref))
    over(2, XE - 2, sweep(yref, zref))


def kernel_a(where, rown, sown, first, second, inverse, g1,
             rhalo, shalo, iext, v, zref, vfirst, vsecond, row, yref, *, n_px, n_py):
    a, b = where[0], where[1]
    even = (a & 1) == 0
    y = iota((T, NZ), 0)

    def start(i, t, rr, ss, inside):
        keep = inside
        if t == 0:
            keep = inside & (b > 0) & (y >= T - HY)
        if t == TILES - 1:
            keep = inside & (b < n_py - 1) & (y < HY)
        inv = jnp.where(keep, 1.0 / (26.0 + ss), 0.0)
        iext[i, tile(t)] = inv
        zref[i, tile(t)] = rr * inv

    def own(i):
        for t in range(TILES):
            start(i, t, rown[i - H, tile(t)], sown[i - H, tile(t)], a >= 0)

    each(H, H + CX, own)
    for t in range(TILES):
        at = tile(t)

        def got(k):
            x, z = first[k, at], second[k, at]
            return jnp.where(even, z, x), jnp.where(even, x, z)

        for k in range(H):
            for i, rr, ss, inside in zip(
                (H - 1 - k, H + CX + k), got(k), got(H + k), (a > 0, a < n_px - 1)
            ):
                at_halo = i if i < H else i - CX
                rhalo[at_halo, at] = rr
                shalo[at_halo, at] = ss
                start(i, t, rr, ss, inside)
    r, s = Field(rown, rhalo), Field(sown, shalo)
    smooth_last(r, iext, zref, yref)

    def apply(i, carry):
        ru, uv, av, sa = carry
        for t, box, mid in neighbours(zref, i, range(TILES)):
            ss = s(i, t)
            vv = (26.0 + ss) * mid - box
            v[i - H, tile(t)] = vv
            if 1 <= t < TILES - 1:
                ru = ru + fold(r(i, t) * mid)
                uv = uv + fold(mid * vv)
                av = av + vv
                sa = sa + ss
        return ru, uv, av, sa

    zero = jnp.zeros((T, LANES), F32)
    wide = jnp.zeros((T, NZ), F32)
    ru, uv, av, sa = lax.fori_loop(H, H + CX, apply, (zero, zero, wide, wide), unroll=UNROLL)
    for k in range(H):
        for t in range(TILES):
            lo, hi = v[k, tile(t)], v[CX - 1 - k, tile(t)]
            vfirst[k, tile(t)] = jnp.where(even, hi, lo)
            vsecond[k, tile(t)] = jnp.where(even, lo, hi)
    lane = iota((1, LANES), 1)
    out = coarse_rows(inverse, g1[...]) + slab_sums(av, AGG) * (1.0 / CELLS)
    out = out + slab_sums(sa, 2 * AGG)
    out = out + jnp.where(lane == 24, total(ru), 0.0) + jnp.where(lane == 25, total(uv), 0.0)
    row[...] = jnp.broadcast_to(out, row.shape)


def kernel_b(where, rown, sown, rhalo, shalo, iext, vown, vfirst, vsecond, inverse, g1, g2,
             rref, qref, zref, vo, row, scal, coarse, yref, rows9, *, n_px, n_py):
    g = g2[...]
    m = g1[...]
    c = line_up(g, 0, n_py)
    shifts = line_up(g, 2 * AGG, n_py)
    w = line_up(g, AGG, n_py)
    lane = iota(g.shape, 1)
    tc = coarse_operator(c, shifts)
    rz = total(jnp.where(lane == 24, g, 0.0)) + CELLS * total(m * c)
    curv = total(jnp.where(lane == 25, g, 0.0)) + total(c * (2.0 * CELLS * w + tc))
    alpha = rz / curv
    e = w + tc * (1.0 / CELLS)
    mnew = m - alpha * e
    coarse[0], coarse[1], coarse[2] = shifts, mnew, e
    cnew = coarse_rows(inverse, mnew)
    planes, boxes = coarse_planes(where, g2, n_px, n_py, rows9)
    r, s = Field(rown, rhalo), Field(sown, shalo)
    even = (where[0] & 1) == 0

    def v(i, t):
        if isinstance(i, int) and not H <= i < H + CX:
            k = H - 1 - i if i < H else i - H - CX
            x, z = vfirst[k, tile(t)], vsecond[k, tile(t)]
            return jnp.where(even, z, x) if i < H else jnp.where(even, x, z)
        return vown[i - H, tile(t)]

    def image(i, pc, bc):
        for t in range(TILES):
            at = tile(t)
            q = v(i, t) + (27.0 + s(i, t)) * pc[at] - bc[at]
            rr = r(i, t) - alpha * q
            qref[i, at] = q
            rref[i, at] = rr
            zref[i, at] = rr * iext[i, at]

    for i in (*range(H + 1), *range(H + CX - 1, XE)):
        block = 0 if i < H else 1 if i < H + CX else 2
        image(i, planes[block], box_plane(boxes, i - H))
    inner = 3.0 * boxes[1]
    each(H + 1, H + CX - 1, lambda i: image(i, planes[1], inner), unroll=7)
    smooth_last(lambda i, t: rref[i, tile(t)], iext, zref, yref)

    def apply(i, carry):
        ru, uv, uq, av = carry
        for t, box, uu in neighbours(zref, i, range(1, TILES - 1)):
            at = tile(t)
            vv = (26.0 + s(i, t)) * uu - box
            vo[i - H, tile(t - 1)] = vv
            ru = ru + fold(rref[i, at] * uu)
            uv = uv + fold(uu * vv)
            uq = uq + fold(uu * qref[i, at])
            av = av + vv
        return ru, uv, uq, av

    zero = jnp.zeros((T, LANES), F32)
    ru, uv, uq, av = lax.fori_loop(
        H, H + CX, apply, (zero, zero, zero, jnp.zeros((T, NZ), F32)), unroll=UNROLL
    )
    lane = iota((1, LANES), 1)
    out = cnew + slab_sums(av, AGG) * (1.0 / CELLS)
    for k, part in ((24, ru), (25, uv), (26, uq)):
        out = out + jnp.where(lane == k, total(part), 0.0)
    row[...] = jnp.broadcast_to(out, row.shape)
    at = iota((8, LANES), 0)
    scal[...] = jnp.where(at == 0, rz, jnp.where(at == 1, curv, alpha))


def kernel_c(where, sown, u, r1, un, vn, q, coarse, g2, g3, scal, x_out, r_out,
             x, r2, rows9, sems, *, n_px, n_py):
    g = g3[...]
    c = line_up(g, 0, n_py)
    w = line_up(g, AGG, n_py)
    lane = iota(g.shape, 1)
    tc = coarse_operator(c, coarse[0])
    rz, curv, alpha = scal[0:1, 0:1], scal[1:2, 0:1], scal[2:3, 0:1]
    rz1 = total(jnp.where(lane == 24, g, 0.0)) + CELLS * total(c * coarse[1])
    zaz = total(jnp.where(lane == 25, g, 0.0)) + total(c * (2.0 * CELLS * w + tc))
    zq = total(jnp.where(lane == 26, g, 0.0)) + CELLS * total(c * coarse[2])
    beta = rz1 / rz
    alpha2 = rz1 / (zaz + 2.0 * beta * zq + beta * beta * curv)
    first = alpha + alpha2 * beta
    planes, boxes = coarse_planes(where, g3, n_px, n_py, rows9)
    me = where[0] * n_py + where[1]
    c_old = spread(jnp.broadcast_to(g2[pl.ds(me, 1), :], (T, LANES)))
    pc = planes[1][T : 2 * T]
    base = first * c_old + alpha2 * pc
    size = CX // PARTS
    copies = []
    for i in range(CX):
        bc = box_plane(boxes, i)
        for t in range(CY // T):
            to, at = tile(t), tile(t + 1)
            x[i, to] = first * u[i + H, at] + alpha2 * un[i + H, at] + base
            image = vn[i, to] + (27.0 + sown[i, at]) * pc - bc[at] + beta * q[i + H, at]
            r2[i, to] = r1[i + H, at] - alpha2 * image
        if (i + 1) % size == 0:
            k = i // size
            for f, (src, dst) in enumerate(((x, x_out), (r2, r_out))):
                part = pl.ds(k * size, size)
                copies.append(
                    pltpu.make_async_copy(src.at[part], dst.at[part], sems.at[f, k])
                )
                copies[-1].start()
    for copy in copies:
        copy.wait()


VMEM = pl.BlockSpec(memory_space=pltpu.VMEM)
SMEM = pl.BlockSpec(memory_space=pltpu.SMEM)
HBM = pl.BlockSpec(memory_space=pltpu.HBM)


def call(body, args, outs, scratch, name, in_specs=None, out_specs=None, **sizes):
    return pl.pallas_call(
        functools.partial(body, **sizes) if sizes else body,
        in_specs=in_specs or [SMEM] + [VMEM] * (len(args) - 1),
        out_specs=out_specs or [VMEM] * len(outs),
        out_shape=[jax.ShapeDtypeStruct(o, F32) for o in outs],
        scratch_shapes=[pltpu.VMEM(x, F32) if isinstance(x, tuple) else x for x in scratch],
        compiler_params=pltpu.CompilerParams(vmem_limit_bytes=32 * 1024 * 1024),
        name=name,
    )(*args)


def swap(x, axis, n, odd):
    pairs = [(i, (i + 1) % n) for i in range(odd, n, 2)]
    return lax.ppermute(x, axis, pairs + [(j, i) for i, j in pairs])


def all_rows(x, axes):
    return lax.all_to_all(x, axes, 0, 0, tiled=True)


def per_device(right_side, shift, coarse_inverse, *, n_px, n_py):
    n = n_px * n_py
    width = n_py * AGG
    sizes = dict(n_px=n_px, n_py=n_py)
    copies = pltpu.SemaphoreType.DMA((2, PARTS))
    where = jnp.stack([lax.axis_index("px"), lax.axis_index("py")]).astype(jnp.int32)
    inputs = [pltpu.with_memory_space_constraint(f, pltpu.HBM) for f in (right_side, shift)]
    face = (2 * CX * HY, NZ)
    r, first, second, row = call(
        kernel_pack_y, (where, *inputs), [OWN, face, face, (n_py, LANES)],
        [(CX, T, NZ), (CX, T, NZ), copies], "pack_y", in_specs=[SMEM, HBM, HBM],
    )
    first = swap(first, "py", n_py, 0)
    second = swap(second, "py", n_py, 1)
    g = all_rows(row, "py")
    face = (2 * H, YE, NZ)
    rown, sown, first, second, row = call(
        kernel_pack_x, (where, r, shift, first, second, g),
        [TALL, TALL, face, face, (n_px, width)], [], "pack_x", n_py=n_py,
    )
    second = swap(second, "px", n_px, 1)
    first = swap(first, "px", n_px, 0)
    g1 = all_rows(row, "px")
    halo = (2 * H, YE, NZ)
    face = (H, YE, NZ)
    rhalo, shalo, iext, v, u, first, second, row = call(
        kernel_a, (where, rown, sown, first, second, coarse_inverse, g1),
        [halo, halo, EXT, TALL, EXT, face, face, (n, LANES)], [EXT], "first", **sizes,
    )
    second = swap(second, "px", n_px, 1)
    first = swap(first, "px", n_px, 0)
    g2 = all_rows(row, ("px", "py"))
    r1, q, un, vn, row, scal, coarse = call(
        kernel_b,
        (where, rown, sown, rhalo, shalo, iext, v, first, second, coarse_inverse, g1, g2),
        [EXT, EXT, EXT, OWN, (n, LANES), (8, LANES), (3, n_px, width)],
        [EXT, (16, LANES)], "second", **sizes,
    )
    g3 = all_rows(row, ("px", "py"))
    return tuple(
        call(
            kernel_c, (where, sown, u, r1, un, vn, q, coarse, g2, g3, scal),
            [OWN, OWN], [OWN, OWN, (16, LANES), copies], "third",
            out_specs=[HBM, HBM], **sizes,
        )
    )


def solution(mesh):
    placed = (P("px", "py", None), P("px", "py", None), P(("px", "py"), None))
    return jax.shard_map(
        functools.partial(per_device, n_px=mesh.shape["px"], n_py=mesh.shape["py"]),
        mesh=mesh,
        in_specs=placed,
        out_specs=(P("px", "py", None), P("px", "py", None)),
        check_vma=False,
    )
```
